32 devices in a mesh: tok: 8 (over z, y), feat: 4 (over x, core).
Axes of the slice: x: 2, y: 2, z: 4, core: 2. Of those that a mesh axis runs over, the one named last changes fastest.
Arguments:
- resid: bfloat16 [1024, 16384], P('feat', 'tok'), may hold values from -6 to 6
- enc_weight: bfloat16 [16384, 11264], P('tok', 'feat'), may hold values from -0.046875 to 0.046875
- enc_bias: float32 [11264], P('feat'), may hold values from -3 to 3
- dec_weight: bfloat16 [11264, 16384], P('feat', 'tok'), may hold values from -0.72 to 0.72
- dec_bias: float32 [16384], P('tok'), may hold values from -2 to 2
- active_ids: int32 [8, 8], P('feat'), may hold values from 0 to 43, as said below
- active_count: int32 [8], P('feat'), may hold values from 4 to 8, as said below
Outputs:
- grad_enc: bfloat16 [16384, 11264], P('tok', 'feat')
- grad_dec: bfloat16 [11264, 16384], P('feat', 'tok')
The draws below stay inside these ranges and needn't reach their ends.
Inputs may be any that keep to these rules, and one draw needn't show every extreme that they name: `active_ids`: entries of one row are distinct. Rows come in aligned runs of 2; in each run, ids of one group h * 11 to h * 11 + 10 stand at most 6 times among all entries, and one group, the same for every run, stands exactly 6 times among the first 4 entries of the run's rows. Token block b uses the first active_count[b] entries of its row.
All inputs are finite; a program needn't handle non-finite values.
Results may differ from the reference program's by a relative error of at most 0.0061.
Values may be sent and summed in bfloat16 or wider, within the bound.
No kernel may reach another device: no remote copies, remote signals or barrier semaphores. Data moves between devices by JAX's collectives and lax.ppermute only.
A program may use at most 256 MiB of HBM per device.

```python
import math
import jax
import jax.numpy as jnp
import numpy as np
from jax import lax

D = 8192
FB = 256
TB = 128
K = 8
LB = 11
TBLK_DEV = 2
NBLK = 44
F = 11264
NTB = 8
TOKENS = 1024
CAP = 6


def draw_active_ids(key, part):
    groups = NBLK // LB
    length = TBLK_DEV * K
    half_slots = K // 2
    front_list = np.array([b * K + s for b in range(TBLK_DEV) for s in range(half_slots)], dtype=np.int32)
    back_list = np.array([b * K + s for b in range(TBLK_DEV) for s in range(half_slots, K)], dtype=np.int32)
    base_labels = np.repeat(np.arange(groups - 1), CAP).astype(np.int32)
    heavy_group = jax.random.randint(jax.random.fold_in(key, 1), (), 0, groups).astype(jnp.int32)

    def source_labels(source_key):
        front_order = jax.random.permutation(jax.random.fold_in(source_key, 2), jnp.asarray(front_list))
        forced = front_order[:CAP]
        spread = jax.random.permutation(jax.random.fold_in(source_key, 3), jnp.concatenate([front_order[CAP:], jnp.asarray(back_list)]))
        others = jnp.asarray(base_labels)
        others = others + (others >= heavy_group).astype(jnp.int32)
        others = jax.random.permutation(jax.random.fold_in(source_key, 4), others)[:length - CAP]
        labels = jnp.zeros((length,), jnp.int32).at[forced].set(heavy_group).at[spread].set(others)
        return labels.reshape(TBLK_DEV, K)
    source_keys = jax.random.split(jax.random.fold_in(key, 5), groups)
    labels = jax.vmap(source_labels)(source_keys).reshape(NTB, K)
    same_group = labels[:, :, None] == labels[:, None, :]
    earlier = jnp.arange(K)[:, None] < jnp.arange(K)[None, :]
    repeat_rank = jnp.sum((same_group & earlier[None]).astype(jnp.int32), axis=1)
    order_keys = jax.random.split(jax.random.fold_in(key, 6), NTB * groups)
    local_orders = jax.vmap(lambda order_key: jax.random.permutation(order_key, LB))(order_keys)
    local_orders = local_orders.reshape(NTB, groups, LB).astype(jnp.int32)
    chosen_row = jnp.take_along_axis(local_orders, labels[:, :, None], axis=1)
    local_pick = jnp.take_along_axis(chosen_row, repeat_rank[:, :, None], axis=2)[:, :, 0]
    return (labels * LB + local_pick).astype(jnp.int32)


def draw_active_count(key, part):
    counts = jax.random.randint(jax.random.fold_in(key, 11), (NTB,), K // 2, K + 1).astype(jnp.int32)
    picked = jax.random.permutation(jax.random.fold_in(key, 12), NTB)[:2]
    counts = counts.at[picked[0]].set(K).at[picked[1]].set(K // 2)
    return counts.astype(jnp.int32)


def draw_dec_weight(key, part):
    full_width = 2 * D
    row_scale = jnp.exp(jax.random.uniform(jax.random.fold_in(key, 21), (F, 1), jnp.float32, math.log(0.3), math.log(3.0)))
    col_scale = jnp.exp(jax.random.uniform(jax.random.fold_in(key, 22), (1, full_width), jnp.float32, math.log(0.5), math.log(2.0)))
    entries = jnp.clip(jax.random.normal(jax.random.fold_in(key, 23), (F, full_width), jnp.float32), -6.0, 6.0)
    return (0.02 * entries * row_scale * col_scale).astype(jnp.bfloat16)


def block_levels(rng, dims, cuts, low, top_value):
    def one(axis_at, blocks):
        heights = jax.random.uniform(jax.random.fold_in(jax.random.fold_in(rng, 6), axis_at), (blocks,), jnp.float32, low / len(cuts), top_value / len(cuts))
        return jnp.repeat(jnp.exp(heights), dims[axis_at] // blocks).reshape((-1,) + (1,) * (len(dims) - axis_at - 1))

    level = one(*cuts[0])
    for cut in cuts[1:]:
        level = level * one(*cut)
    return level


def gaussian(rng, dims, width, reach, cuts=(), kind=jnp.bfloat16):
    result = width * jax.random.normal(rng, dims, jnp.float32)
    if cuts:
        result = result * block_levels(rng, dims, cuts, -0.22, 0.18)
    return jnp.clip(result, -reach, reach).astype(kind)


def setup_inputs(seed: int = 0) -> dict:
    seeds = jax.random.split(jax.random.key(seed), 8)
    return {
        "resid": gaussian(seeds[0], (TOKENS, 2 * D), 1.0, 6.0, ((0, 4), (1, 8))),
        "enc_weight": gaussian(seeds[1], (2 * D, F), (2 * D) ** -0.5, 0.046875, ((0, 8), (1, 4))),
        "enc_bias": gaussian(seeds[2], (F,), 0.5, 3.0, ((0, 4),), jnp.float32),
        "dec_weight": draw_dec_weight(jax.random.fold_in(seeds[7], 71), 0),
        "dec_bias": gaussian(seeds[4], (2 * D,), 0.3, 2.0, ((0, 8),), jnp.float32),
        "active_ids": draw_active_ids(jax.random.fold_in(seeds[7], 71), 0),
        "active_count": draw_active_count(jax.random.fold_in(seeds[7], 71), 0),
    }


norm_eps = 1e-06
sparsity_weight = 0.2

def reference(resid, enc_weight, enc_bias, dec_weight, dec_bias, active_ids, active_count):
    full_width = 2 * D
    blocks = resid.reshape(NTB, TB, full_width)
    dec_blocks = dec_weight.reshape(NBLK, FB, full_width)

    def block_norms(block):
        squared = block.astype(jnp.float32) ** 2
        return jnp.stack([lax.optimization_barrier(jnp.sum(squared[:, :D], axis=1)), lax.optimization_barrier(jnp.sum(squared[:, D:], axis=1))])
    norm_pairs = jnp.sqrt(lax.map(block_norms, dec_blocks) + norm_eps)
    dec_norm = lax.optimization_barrier(jnp.sum(norm_pairs, axis=1))
    inv_norm = 1.0 / norm_pairs
    is_live = jnp.arange(K)[None, :] < active_count[:, None]

    def forward(inputs):
        token_rows, block_ids, live_row = inputs
        rebuilt = jnp.zeros((TB, full_width), jnp.float32)
        act_list = []
        positive_list = []
        for slot_index in range(K):
            block = block_ids[slot_index].astype(jnp.int32)
            columns = lax.dynamic_slice_in_dim(enc_weight, block * FB, FB, 1)
            preact = jnp.dot(token_rows, columns, preferred_element_type=jnp.float32)
            preact = preact + lax.dynamic_slice_in_dim(enc_bias, block * FB, FB, 0)[None, :]
            positive = jnp.maximum(preact, 0.0)
            acts = jnp.where(live_row[slot_index], positive * positive, 0.0).astype(jnp.bfloat16)
            recon_part = jnp.dot(acts, dec_blocks[block], preferred_element_type=jnp.float32).astype(jnp.bfloat16)
            recon_part = lax.optimization_barrier(recon_part)
            rebuilt = rebuilt + recon_part.astype(jnp.float32)
            act_list.append(acts)
            positive_list.append(positive)
        return (rebuilt, jnp.stack(act_list), jnp.stack(positive_list))
    rebuilt, all_acts, positives = lax.map(forward, (blocks, active_ids, is_live))
    errors = rebuilt + dec_bias[None, None, :] - blocks.astype(jnp.float32)
    out_grad = (errors * TB ** (-0.5)).astype(jnp.bfloat16)

    def backward(inputs):
        grad_rows, block_ids, live_row, positive_rows = inputs
        grad_list = []
        for slot_index in range(K):
            block = block_ids[slot_index].astype(jnp.int32)
            act_grad = jnp.dot(grad_rows, dec_blocks[block].T, preferred_element_type=jnp.float32)
            act_grad = act_grad + sparsity_weight * dec_norm[block][None, :]
            grad_list.append(jnp.where(live_row[slot_index], act_grad * 2.0 * positive_rows[slot_index], 0.0).astype(jnp.bfloat16))
        return jnp.stack(grad_list)
    preact_grads = lax.map(backward, (out_grad, active_ids, is_live, positives))
    flat_ids = active_ids.reshape(-1).astype(jnp.int32)
    pair_order = jnp.argsort(flat_ids, stable=True).astype(jnp.int32)
    column_index = jnp.arange(full_width)[None, :]
    zero_index = jnp.int32(0)

    def accumulate(carry, pair):
        out_enc, out_dec, sum_enc, sum_dec, previous = carry
        token_index = pair // K
        slot_index = pair % K
        block = flat_ids[pair]
        acts = all_acts[token_index, slot_index]
        enc_term = jnp.dot(blocks[token_index].T, preact_grads[token_index, slot_index], preferred_element_type=jnp.float32)
        inv_cols = jnp.where(column_index < D, inv_norm[block, 0][:, None], inv_norm[block, 1][:, None])
        dec_term = jnp.dot(acts.T, out_grad[token_index], preferred_element_type=jnp.float32)
        dec_term = dec_term + sparsity_weight * lax.optimization_barrier(jnp.sum(acts.astype(jnp.float32), axis=0))[:, None] * dec_blocks[block].astype(jnp.float32) * inv_cols
        fresh = block != previous
        sum_enc = jnp.where(fresh, 0.0, sum_enc) + enc_term
        sum_dec = jnp.where(fresh, 0.0, sum_dec) + dec_term
        out_enc = lax.dynamic_update_slice(out_enc, sum_enc.astype(jnp.bfloat16)[:, None, :], (zero_index, block, zero_index))
        out_dec = lax.dynamic_update_slice(out_dec, sum_dec.astype(jnp.bfloat16)[None], (block, zero_index, zero_index))
        return ((out_enc, out_dec, sum_enc, sum_dec, block), None)
    start = (jnp.zeros((full_width, NBLK, FB), jnp.bfloat16), jnp.zeros((NBLK, FB, full_width), jnp.bfloat16), jnp.zeros((full_width, FB), jnp.float32), jnp.zeros((FB, full_width), jnp.float32), jnp.int32(-1))
    final, _ = lax.scan(accumulate, start, pair_order)
    return (final[0].reshape(full_width, F), final[1].reshape(F, full_width))
```

```python
import functools

import jax
import jax.numpy as jnp
from jax import lax
from jax.experimental import pallas as pl
from jax.experimental.pallas import tpu as pltpu
from jax.sharding import PartitionSpec as P

D = 8192
FB = 256
TB = 128
K = 8
LB = 11


norm_eps = 1e-06
sparsity_weight = 0.2
GRAIN = 16
VMEM = 24 * 2**20
DEPTH = 6

f32 = jnp.float32
bf16 = jnp.bfloat16


def swap(value, axis, mask):
    size = lax.axis_size(axis)
    return lax.ppermute(value, axis, [(i, i ^ mask) for i in range(size)])


def full(shape):
    return pl.BlockSpec(shape, lambda *_: (0,) * len(shape), pipeline_mode=pl.Buffered(1))


def like(shape, dtype=bf16):
    return jax.ShapeDtypeStruct(tuple(shape), dtype)


class Plan:
    def __init__(self, groups, toks, rows, columns):
        self.groups, self.toks, self.rows, self.columns = groups, toks, rows, columns
        self.chips = groups // 2
        self.line = toks // 2
        self.blocks = rows // TB
        self.cap = (3 * self.blocks * K + 2 * groups - 1) // (2 * groups)
        unit = max(2, toks * GRAIN // TB)
        self.slots = -(-2 * self.cap // unit) * unit
        self.half = self.slots // 2
        self.shard = self.slots * TB // toks
        self.block = self.slots
        self.live = 2 * self.slots
        self.pair = 3 * self.slots
        self.place = self.pair + 1
        self.size = self.pair + 2
        self.every = self.chips * self.slots
        self.start = 2 * self.every
        self.cursor = self.start + LB + 1
        self.pair_all = self.cursor + LB
        self.place_all = self.pair_all + 1
        self.size_all = self.pair_all + 2
        self.trail = []

    def pin(self, value):
        return lax.optimization_barrier((value, self.trail))[0]

    def launch(
        self, kernel, name, grid, tab, ins, outs, scratch=(), into=None
    ):
        arrays, specs = [tab], []
        for value, spec in ins:
            arrays.append(value)
            specs.append(full(value.shape) if spec is None else spec)
        extra = list(self.trail) if into is None else [into, *self.trail]
        count = len(specs)

        def body(tab, *refs):
            kernel(tab, *refs[:count], *refs[count + len(extra) :])

        made = pl.pallas_call(
            body,
            grid_spec=pltpu.PrefetchScalarGridSpec(
                num_scalar_prefetch=1,
                grid=grid,
                in_specs=specs + [pl.BlockSpec(memory_space=pl.ANY)] * len(extra),
                out_specs=[full(shape.shape) if spec is None else spec for shape, spec in outs],
                scratch_shapes=list(scratch),
            ),
            out_shape=[shape for shape, _ in outs],
            input_output_aliases={} if into is None else {count + 1: 0},
            compiler_params=pltpu.CompilerParams(vmem_limit_bytes=VMEM),
            cost_estimate=pl.CostEstimate(flops=1, bytes_accessed=1, transcendentals=0),
            name=name,
        )(*arrays, *extra)
        self.trail = [made[-1]]
        return made


def table_kernel(plan, ids_near, ids_far, tab):
    feat, tok = lax.axis_index("feat"), lax.axis_index("tok")
    tab[plan.pair] = tok % 2
    tab[plan.place] = tok // 2
    last = jnp.int32(0)
    for core, ids in enumerate((ids_near, ids_far)):
        base = core * plan.cap

        def entry(i, carry):
            used, last = carry
            name = ids[i // K, i % K]
            hit = (name >= feat * LB) & (name < feat * LB + LB)
            local = jnp.where(hit, name - feat * LB, last)

            @pl.when(hit)
            def _():
                tab[base + used] = core * plan.blocks + i // K
                tab[plan.block + base + used] = local
                tab[plan.live + base + used] = 1

            return used + hit.astype(jnp.int32), local

        used, last = lax.fori_loop(0, plan.blocks * K, entry, (jnp.int32(0), last))

        def empty(i, last):
            tab[base + i] = core * plan.blocks
            tab[plan.block + base + i] = last
            tab[plan.live + base + i] = 0
            return last

        lax.fori_loop(used, plan.cap if core == 0 else plan.slots - plan.cap, empty, last)


def slot_table(plan, ids):
    smem = pl.BlockSpec(memory_space=pltpu.SMEM)
    tab = pl.pallas_call(
        functools.partial(table_kernel, plan),
        out_shape=like((plan.size,), jnp.int32),
        in_specs=[smem] * 2,
        out_specs=smem,
        name="slot_table",
    )(*ids)
    plan.trail = [tab]
    return tab


def order_kernel(plan, *refs):
    tabs, every = refs[:-1], refs[-1]
    every[plan.pair_all] = tabs[0][plan.pair]
    every[plan.place_all] = tabs[0][plan.place]
    for i in range(LB + 1):
        every[plan.start + i] = 0
    for tab in tabs:

        def count(i, carry):
            at = plan.start + tab[plan.block + i] + 1
            every[at] = every[at] + tab[plan.live + i]
            return carry

        lax.fori_loop(0, plan.slots, count, 0)
    for i in range(LB):
        every[plan.start + i + 1] = every[plan.start + i] + every[plan.start + i + 1]
        every[plan.cursor + i] = every[plan.start + i]
    for chunk, tab in enumerate(tabs):

        def put(i, carry):
            @pl.when(tab[plan.live + i] > 0)
            def _():
                block = tab[plan.block + i]
                at = every[plan.cursor + block]
                every[at] = chunk * plan.slots + i
                every[plan.every + at] = chunk * 2 * plan.blocks + tab[i]
                every[plan.cursor + block] = at + 1

            return carry

        lax.fori_loop(0, plan.slots, put, 0)


def order_table(plan, tabs):
    smem = pl.BlockSpec(memory_space=pltpu.SMEM)
    every = pl.pallas_call(
        functools.partial(order_kernel, plan),
        out_shape=like((plan.size_all,), jnp.int32),
        in_specs=[smem] * len(tabs),
        out_specs=smem,
        name="order_table",
    )(*[plan.pin(tab) for tab in tabs])
    plan.trail = [every]
    return every


def block_copy(tab, at, weight, decoder, held, sems, i):
    rows = pl.ds(pl.multiple_of(tab[at] * FB, FB), FB)
    source = weight.at[rows, :] if decoder else weight.at[:, rows]
    return pltpu.make_async_copy(source, held.at[i], sems.at[i])


def half_loop(plan, own, decoder, tab, rows, weight, out, held, sems):
    base = (tab[plan.pair] if own else 1 - tab[plan.pair]) * plan.half

    def copy(i):
        return block_copy(tab, plan.block + base + i, weight, decoder, held, sems, i)

    def start(i, carry):
        @pl.when(tab[plan.live + base + i] > 0)
        def _():
            copy(i).start()

        return carry

    def multiply(i, carry):
        live = tab[plan.live + base + i] > 0
        token = tab[base + i]
        to = pl.ds(pl.multiple_of(i * TB, TB), TB)

        @pl.when(live)
        def _():
            copy(i).wait()

        every = rows[0].shape[0] // TB
        for core, ref in enumerate(rows):

            @pl.when(live & (token // every == core))
            def _():
                at = pl.ds(pl.multiple_of((token % every) * TB, TB), TB)
                out[to, :] = lax.dot_general(
                    ref[at, :],
                    held[i],
                    (((1,), (1 if decoder else 0,)), ((), ())),
                    preferred_element_type=f32,
                ).astype(out.dtype)

        @pl.when(jnp.logical_not(live))
        def _():
            out[to, :] = jnp.zeros((TB, FB), out.dtype)

        return carry

    return start, multiply


def run_half(plan, own, decoder, tab, rows, weight, out, held, sems):
    start, multiply = half_loop(plan, own, decoder, tab, rows, weight, out, held, sems)
    lax.fori_loop(0, plan.half, start, 0)
    lax.fori_loop(0, plan.half, multiply, 0)


def hbm():
    return pl.BlockSpec(memory_space=pltpu.HBM)


def half_scratch(plan, decoder):
    shape = (FB, plan.columns) if decoder else (plan.columns, FB)
    return [pltpu.VMEM((plan.half, *shape), bf16), pltpu.SemaphoreType.DMA((plan.half,))]


def preact_kernel(plan, own, tab, near, far, weight, out, held, sems):
    run_half(plan, own, False, tab, (near, far), weight, out, held, sems)


def preact_half(plan, own, tab, near, far, weight):
    return plan.launch(
        functools.partial(preact_kernel, plan, own),
        "preact_half",
        (1,),
        tab,
        [(near, None), (far, None), (weight, hbm())],
        [(like((plan.half * TB, FB), f32 if own else bf16), None)],
        half_scratch(plan, False),
    )[0]


def act_send_kernel(plan, tab, weight, near, *refs):
    parts, (errs, out, held, sems) = refs[:-4], refs[-4:]
    start, multiply = half_loop(plan, False, True, tab, (errs,), weight, out, held, sems)
    lax.fori_loop(0, plan.half, start, 0)
    errs[: plan.rows, :] = near[...]
    size = plan.rows // len(parts)
    for i, part in enumerate(parts):
        errs[plan.rows + i * size : plan.rows + (i + 1) * size, :] = part[...]
    lax.fori_loop(0, plan.half, multiply, 0)


def chunk_rows(plan, chunk):
    return pl.BlockSpec(
        (2 * plan.rows, plan.columns), lambda *_: (chunk, 0), pipeline_mode=pl.Buffered(1)
    )


def act_send(plan, chunk, tab, near, parts, weight, errs):
    return plan.launch(
        functools.partial(act_send_kernel, plan),
        "act_grad_send",
        (1,),
        tab,
        [(weight, hbm()), (near, None)] + [(part, None) for part in parts],
        [
            (like((plan.chips * 2 * plan.rows, plan.columns)), chunk_rows(plan, chunk)),
            (like((plan.half * TB, FB)), None),
        ],
        half_scratch(plan, True),
        into=errs,
    )


def act_keep_kernel(plan, tab, weight, errs, out, held, sems):
    run_half(plan, True, True, tab, (errs,), weight, out, held, sems)


def act_keep(plan, chunk, tab, errs, weight):
    return plan.launch(
        functools.partial(act_keep_kernel, plan),
        "act_grad_keep",
        (1,),
        tab,
        [(weight, hbm()), (errs, chunk_rows(plan, chunk))],
        [(like((plan.half * TB, FB), f32), None)],
        half_scratch(plan, True),
    )[0]


def pair_sum_kernel(plan, tab, keep, recv, *outs):
    for i, out in enumerate(outs):
        at = pl.multiple_of((tab[plan.place] ^ i) * plan.shard, GRAIN)
        rows = pl.ds(at, plan.shard)
        out[...] = (keep[rows, :] + recv[rows, :].astype(f32)).astype(out.dtype)


def pair_sum(plan, tab, keep, recv):
    shape = (plan.shard, FB)
    return plan.launch(
        functools.partial(pair_sum_kernel, plan),
        "pair_sum",
        (1,),
        tab,
        [(keep, None), (recv, None)],
        [(like(shape, bf16 if i else f32), None) for i in range(plan.line)],
    )


def grain_slot(plan, tab, grain):
    shard = tab[plan.pair] * plan.line + tab[plan.place]
    slot = (shard * plan.shard + grain * GRAIN) // TB
    return tab[plan.block + slot], tab[plan.live + slot] > 0


def act_kernel(plan, tab, bias, *refs):
    parts, (acts, positives) = refs[:-2], refs[-2:]
    for grain in range(plan.shard // GRAIN):
        block, live = grain_slot(plan, tab, grain)
        rows = slice(grain * GRAIN, (grain + 1) * GRAIN)
        total = bias[pl.ds(block, 1), :]
        for part in parts:
            total = total + part[rows, :].astype(f32)
        positive = jnp.where(live, jnp.maximum(total, 0.0), 0.0)
        positives[rows, :] = positive
        acts[rows, :] = (positive * positive).astype(bf16)


def shard_acts(plan, tab, bias, parts):
    shape = (plan.shard, FB)
    return plan.launch(
        functools.partial(act_kernel, plan),
        "shard_acts",
        (1,),
        tab,
        [(bias, None)] + [(part, None) for part in parts],
        [(like(shape), None), (like(shape, f32), None)],
    )


def grad_kernel(plan, tab, norms, positives, *refs):
    parts, out = refs[:-1], refs[-1]
    for grain in range(plan.shard // GRAIN):
        block, live = grain_slot(plan, tab, grain)
        rows = slice(grain * GRAIN, (grain + 1) * GRAIN)
        total = sparsity_weight * norms[pl.ds(block, 1), :]
        for part in parts:
            total = total + part[rows, :].astype(f32)
        out[rows, :] = jnp.where(live, total * 2.0 * positives[rows, :], 0.0).astype(bf16)


def shard_grads(plan, tab, norms, positives, parts):
    return plan.launch(
        functools.partial(grad_kernel, plan),
        "shard_grads",
        (1,),
        tab,
        [(norms, None), (positives, None)] + [(part, None) for part in parts],
        [(like((plan.shard, FB)), None)],
    )[0]


def assemble(plan, pair, place, near, far, out, base):
    for side, ref in enumerate((near, far)):
        for i in range(plan.line):
            shard = (pair ^ side) * plan.line + (place ^ i)
            at = pl.multiple_of(base + shard * plan.shard, GRAIN)
            out[pl.ds(at, plan.shard), :] = ref[i * plan.shard : (i + 1) * plan.shard, :]


def recon_kernel(plan, tab, near, far, weight, acts, own, *refs):
    others, (total, held, sems) = refs[:-3], refs[-3:]
    depth = held.shape[0]

    def copy(i):
        return block_copy(tab, plan.block + i, weight, True, held, sems, i % depth)

    def start(i, carry):
        @pl.when(tab[plan.live + i] > 0)
        def _():
            copy(i).start()

        return carry

    def multiply(i, carry):
        @pl.when(tab[plan.live + i] > 0)
        def _():
            at = pl.ds(pl.multiple_of(tab[i] * TB, TB), TB)
            rows = pl.ds(pl.multiple_of(i * TB, TB), TB)
            copy(i).wait()
            total[at, :] += jnp.dot(acts[rows, :], held[i % depth], preferred_element_type=f32)

        @pl.when(i + depth < plan.slots)
        def _():
            start(i + depth, 0)

        return carry

    lax.fori_loop(0, depth, start, 0)
    assemble(plan, tab[plan.pair], tab[plan.place], near, far, acts, 0)
    total[...] = jnp.zeros_like(total)
    lax.fori_loop(0, plan.slots, multiply, 0)
    own[...] = total[: plan.rows, :]
    size = plan.rows // len(others)
    for i, other in enumerate(others):
        other[...] = total[plan.rows + i * size : plan.rows + (i + 1) * size, :].astype(bf16)


def recon(plan, chunk, tab, near, far, dec_weight, acts, pieces):
    depth = min(DEPTH, plan.slots)
    acts_shape = (plan.slots * TB, FB)
    piece = like((plan.rows // pieces, plan.columns))
    return plan.launch(
        functools.partial(recon_kernel, plan),
        "recon",
        (1,),
        tab,
        [(near, None), (far, None), (dec_weight, hbm())],
        [
            (
                like((plan.every * TB, FB)),
                pl.BlockSpec(acts_shape, lambda *_: (chunk, 0), pipeline_mode=pl.Buffered(1)),
            ),
            (like((plan.rows, plan.columns), f32), None),
        ]
        + [(piece, None)] * pieces,
        [
            pltpu.VMEM((2 * plan.rows, plan.columns), f32),
            pltpu.VMEM((depth, FB, plan.columns), bf16),
            pltpu.SemaphoreType.DMA((depth,)),
        ],
        into=acts,
    )


def column(row):
    return jnp.broadcast_to(row, (TB, row.shape[1])).T[:, :1]


def square_kernel(tab, weight, out):
    value = weight[...].astype(f32)
    total = jnp.sum(value * value, axis=1, keepdims=True)
    out[...] = jnp.broadcast_to(total, (FB, TB)).T[:8, :].reshape(1, 8, FB)


def square_sums(plan, tab, dec_weight):
    return plan.launch(
        square_kernel,
        "square_sums",
        (LB,),
        tab,
        [(dec_weight, pl.BlockSpec((FB, plan.columns), lambda i, tab: (i, 0)))],
        [(like((LB, 8, FB), f32), pl.BlockSpec((1, 8, FB), lambda i, tab: (i, 0, 0)))],
    )[0][:, 0, :]


def turn_kernel(tab, near, far, out):
    rows = near.shape[0]
    out[:, :rows] = near[...].T
    out[:, rows:] = far[...].T


def turned(plan, chunk, tab, near, far, into):
    width = min(512, plan.columns)
    block = pl.BlockSpec((plan.rows, width), lambda i, tab: (0, i))
    return plan.launch(
        turn_kernel,
        "turn_rows",
        (plan.columns // width,),
        tab,
        [(near, block), (far, block)],
        [
            (
                pltpu.HBM((plan.columns, plan.chips * 2 * plan.rows), bf16),
                pl.BlockSpec((width, 2 * plan.rows), lambda i, tab: (i, chunk)),
            )
        ],
        into=into,
    )[0]


def norm_add_kernel(tab, here, there, out):
    out[...] = here[...] + there[...]


def norm_add(plan, tab, here, there):
    return plan.launch(
        norm_add_kernel,
        "norm_add",
        (1,),
        tab,
        [(here, None), (there, None)],
        [(like(here.shape, f32), None)],
    )[0]


def norm_kernel(tab, here, there, total, inverse):
    norm = jnp.sqrt(here[...] + norm_eps)
    total[...] = norm + jnp.sqrt(there[...] + norm_eps)
    inverse[...] = 1.0 / norm


def norms(plan, tab, here, there):
    return plan.launch(
        norm_kernel,
        "norms",
        (1,),
        tab,
        [(here, None), (there, None)],
        [(like(here.shape, f32), None)] * 2,
    )


def two_slots(tab, plan, i, last):
    more = i + 1 < last
    j = jnp.where(more, i + 1, i)

    def at(value):
        return pl.ds(pl.multiple_of(value * TB, TB), TB)

    return more, at(tab[i]), at(tab[j]), at(tab[plan.every + i]), at(tab[plan.every + j])


def grad_dec_kernel(plan, base, tab, inverse, weight, acts, errs, out, mark, total, sums):
    mark[...] = jnp.zeros_like(mark)
    block = base + pl.program_id(0)
    first, last = tab[plan.start + block], tab[plan.start + block + 1]

    def load(i):
        more, here, there, token, other = two_slots(tab, plan, i, last)
        second = jnp.where(more, acts[there, :], jnp.zeros((TB, FB), bf16))
        these = jnp.concatenate([acts[here, :], second], axis=0).T
        rows = jnp.concatenate([errs[token, :], errs[other, :]], axis=0)
        count = jnp.dot(these, jnp.ones((2 * TB, TB), bf16), preferred_element_type=f32)
        return count, jnp.dot(these, rows, preferred_element_type=f32)

    def finish(count, value):
        scale = sparsity_weight * count[:, :1] * column(inverse[pl.ds(block, 1), :])
        out[...] = (value + scale * weight[...].astype(f32)).astype(bf16)

    @pl.when((last > first) & (last - first <= 2))
    def _():
        finish(*load(first))

    @pl.when(last - first > 2)
    def _():
        count, value = load(first)
        sums[...] = count
        total[...] = value

        def add(i, carry):
            count, value = load(first + 2 * i)
            sums[...] += count
            total[...] += value
            return carry

        lax.fori_loop(1, (last - first + 1) // 2, add, 0)
        finish(sums[...], total[...])

    @pl.when(first >= last)
    def _():
        out[...] = jnp.zeros(out.shape, bf16)


def grad_dec(plan, base, count, tab, inverse, dec_weight, acts, errs, into=None):
    shape = (FB, plan.columns)
    spec = pl.BlockSpec(shape, lambda i, tab: (base + i, 0))
    return plan.launch(
        functools.partial(grad_dec_kernel, plan, base),
        "grad_dec",
        (count,),
        tab,
        [(inverse, None), (dec_weight, spec), (acts, None), (errs, None)],
        [(like((LB * FB, plan.columns)), spec), (like((8, TB), f32), None)],
        [pltpu.VMEM(shape, f32), pltpu.VMEM((FB, TB), f32)],
        into=into,
    )[0]


def grad_enc_kernel(plan, tab, rows, *refs):
    grads, (out, total, every) = refs[: 2 * plan.chips], refs[2 * plan.chips :]
    block = pl.program_id(0)

    @pl.when(block == 0)
    def _():
        for chunk in range(plan.chips):
            near, far = grads[2 * chunk], grads[2 * chunk + 1]
            base = chunk * plan.slots * TB
            assemble(plan, tab[plan.pair_all], tab[plan.place_all], near, far, every, base)

    first, last = tab[plan.start + block], tab[plan.start + block + 1]

    def load(i):
        more, here, there, token, other = two_slots(tab, plan, i, last)
        second = jnp.where(more, every[there, :], jnp.zeros((TB, FB), bf16))
        right = jnp.concatenate([every[here, :], second], axis=0)
        left = jnp.concatenate([rows[:, token], rows[:, other]], axis=1)
        return jnp.dot(left, right, preferred_element_type=f32)

    @pl.when(last - first > 2)
    def _():
        total[...] = load(first)

        def add(i, carry):
            total[...] += load(first + 2 * i)
            return carry

        lax.fori_loop(1, (last - first + 1) // 2, add, 0)
        out[...] = total[...].astype(bf16)

    @pl.when((last > first) & (last - first <= 2))
    def _():
        out[...] = load(first).astype(bf16)

    @pl.when(last == first)
    def _():
        out[...] = jnp.zeros(out.shape, bf16)


def grad_enc(plan, tab, grads, rows):
    shape = (plan.columns, FB)
    return plan.launch(
        functools.partial(grad_enc_kernel, plan),
        "grad_enc",
        (LB,),
        tab,
        [(value, None) for value in (rows, *grads)],
        [(like((plan.columns, LB * FB)), pl.BlockSpec(shape, lambda i, tab: (0, i)))],
        [pltpu.VMEM(shape, f32), pltpu.VMEM((plan.every * TB, FB), bf16)],
    )[0]


def join_kernel(tab, *refs):
    out = refs[-1]
    for i, ref in enumerate(refs[:-1]):
        out[i * ref.shape[0] : (i + 1) * ref.shape[0], :] = ref[...]


def join(plan, tab, parts):
    return plan.launch(
        join_kernel,
        "join_shards",
        (1,),
        tab,
        [(part, None) for part in parts],
        [(like((plan.half * TB, FB)), None)],
    )[0]


def chip_sum_kernel(tab, own, *refs):
    others, (total, rounded) = refs[:-2], refs[-2:]
    size = others[0].shape[0]
    for i, other in enumerate(others):
        at = slice(i * size, (i + 1) * size)
        value = own[at, :] + other[...].astype(f32)
        total[at, :] = value
        rounded[at, :] = value.astype(bf16)


def chip_sum(plan, tab, own, others):
    return plan.launch(
        chip_sum_kernel,
        "chip_sum",
        (1,),
        tab,
        [(own, None)] + [(other, None) for other in others],
        [(like(own.shape, f32), None), (like(own.shape), None)],
    )


def error_kernel(pieces, tab, total, bias, rows, *refs):
    others, near, parts = refs[: -1 - pieces], refs[-1 - pieces], refs[-pieces:]
    size = parts[0].shape[0]
    for i, part in enumerate(parts):
        at = slice(i * size, (i + 1) * size)
        value = total[at, :]
        for other in others:
            value = value + other[at, :].astype(f32)
        error = value + bias[...] - rows[at, :].astype(f32)
        error = (error * TB ** (-0.5)).astype(bf16)
        near[at, :] = error
        part[...] = error


def errors(plan, tab, total, bias, rows, received, pieces):
    piece = like((plan.rows // pieces, plan.columns))
    return plan.launch(
        functools.partial(error_kernel, pieces),
        "errors",
        (1,),
        tab,
        [(total, None), (bias, None), (rows, None)] + [(value, None) for value in received],
        [(like(rows.shape), None)] + [(piece, None)] * pieces,
    )


def spread_parts(plan, parts):
    return [parts[0]] + [swap(parts[i], "tok", 2 * i) for i in range(1, plan.line)]


def spread_shard(plan, shard):
    return [shard] + [swap(shard, "tok", 2 * i) for i in range(1, plan.line)]


def on_device(resid, enc_weight, enc_bias, dec_weight, dec_bias, active_ids, active_count):
    plan = Plan(lax.axis_size("feat"), lax.axis_size("tok"), *resid.shape)
    chips = range(plan.chips)
    rest = list(chips[1:])
    enc_weight = pltpu.with_memory_space_constraint(enc_weight, pltpu.HBM)
    dec_weight = pltpu.with_memory_space_constraint(dec_weight, pltpu.HBM)
    bias = enc_bias.reshape(LB, FB)
    back = dec_bias[None, :]

    def from_chip(value, chunk):
        return swap(value, "feat", 2 * chunk)

    def both(value):
        return value, swap(value, "feat", 1)

    entries = jnp.where(jnp.arange(K)[None, :] < active_count[:, None], active_ids, -1)
    lists = {chunk: from_chip(entries, chunk) for chunk in rest}
    tabs = {0: slot_table(plan, both(entries))}
    rows = {0: both(resid)}
    arriving = {}
    for chunk in rest:
        lists[chunk], mine = lax.optimization_barrier((lists[chunk], resid))
        arriving[chunk] = from_chip(mine, chunk)
    sends, keeps, parts, shards, positives, sums, received, fresh = ({} for _ in range(8))
    turns = acts = errs = None

    def products(chunk):
        tab, (near, far) = tabs[chunk], rows[chunk]
        sends[chunk] = swap(preact_half(plan, False, tab, near, far, enc_weight), "tok", 1)
        keeps[chunk] = preact_half(plan, True, tab, near, far, enc_weight)

    def reduce_pairs(chunk):
        parts[chunk] = spread_parts(plan, pair_sum(plan, tabs[chunk], keeps[chunk], sends[chunk]))

    def activate(chunk):
        shard, positives[chunk] = shard_acts(plan, tabs[chunk], bias, parts[chunk])
        shards[chunk] = spread_shard(plan, shard)

    def gather(chunk):
        near = join(plan, tabs[chunk], shards[chunk])
        shards[chunk] = (near, swap(near, "tok", 1))

    def rebuild(chunk, acts):
        acts, own, *others = recon(plan, chunk, tabs[chunk], *shards[chunk], dec_weight, acts, 4 if chunk else 16)
        sums[chunk] = (own, [swap(other, "feat", 1) for other in others])
        return acts

    def total(chunk):
        sums[chunk], rounded = chip_sum(plan, tabs[chunk], *sums[chunk])
        for step in rest:
            received[chunk ^ step, step] = from_chip(rounded, step)

    def compare(chunk):
        others = [received[chunk, step] for step in rest]
        near, *pieces = errors(plan, tabs[chunk], sums[chunk], back, rows[chunk][0], others, 4 if chunk else 16)
        fresh[chunk] = (near, [swap(piece, "feat", 1) for piece in pieces])

    def back_products(chunk, errs):
        errs, send = act_send(plan, chunk, tabs[chunk], *fresh[chunk], dec_weight, errs)
        sends[chunk] = swap(send, "tok", 1)
        keeps[chunk] = act_keep(plan, chunk, tabs[chunk], errs, dec_weight)
        return errs

    def differentiate(chunk):
        shard = shard_grads(plan, tabs[chunk], norm_sum, positives[chunk], parts[chunk])
        shards[chunk] = spread_shard(plan, shard)

    products(0)
    for chunk in rest:
        tabs[chunk] = slot_table(plan, both(plan.pin(lists[chunk])))
    reduce_pairs(0)
    turns = turned(plan, 0, tabs[0], *rows[0], turns)
    activate(0)
    for chunk in rest:
        rows[chunk] = both(plan.pin(arriving[chunk]))
        near, far = rows[chunk]
        sends[chunk] = swap(preact_half(plan, False, tabs[chunk], near, far, enc_weight), "tok", 1)
    gather(0)
    for chunk in rest:
        near, far = rows[chunk]
        keeps[chunk] = preact_half(plan, True, tabs[chunk], near, far, enc_weight)
        turns = turned(plan, chunk, tabs[chunk], *rows[chunk], turns)
        reduce_pairs(chunk)
    acts = rebuild(0, acts)
    for chunk in rest:
        activate(chunk)
    total(0)
    order = order_table(plan, [tabs[chunk] for chunk in chips])
    for chunk in rest:
        gather(chunk)
    squares = square_sums(plan, tabs[0], dec_weight)
    for chunk in rest:
        acts = rebuild(chunk, acts)
        total(chunk)

    bits = [1 << i for i in range((plan.toks - 1).bit_length())]
    for chunk in rest:
        compare(chunk)
        errs = back_products(chunk, errs)
        reduce_pairs(chunk)
    squares = norm_add(plan, tabs[0], squares, swap(squares, "tok", 1))
    compare(0)
    errs = back_products(0, errs)
    for bit in bits[1:-1]:
        squares = norm_add(plan, tabs[0], squares, swap(squares, "tok", bit))
    norm_sum, inverse = norms(plan, tabs[0], squares, swap(squares, "tok", bits[-1]))
    for chunk in rest:
        differentiate(chunk)
    values = (order, inverse, dec_weight, acts, errs)
    reduce_pairs(0)
    out_dec = grad_dec(plan, 0, 4, *values)
    for chunk in rest:
        gather(chunk)
    differentiate(0)
    out_dec = grad_dec(plan, 4, 4, *values, into=out_dec)
    gather(0)
    out_dec = grad_dec(plan, 8, LB - 8, *values, into=out_dec)
    out_enc = grad_enc(plan, order, [piece for chunk in chips for piece in shards[chunk]], turns)
    return (out_enc, out_dec)


def solution(mesh):
    return jax.shard_map(
        on_device,
        mesh=mesh,
        in_specs=(
            P("feat", "tok"),
            P("tok", "feat"),
            P("feat"),
            P("feat", "tok"),
            P("tok"),
            P("feat", None),
            P("feat"),
        ),
        out_specs=(P("tok", "feat"), P("feat", "tok")),
        check_vma=False,
    )
```

```python
import functools

import jax
import jax.numpy as jnp
from jax import lax
from jax.experimental import pallas as pl
from jax.experimental.pallas import tpu as pltpu
from jax.sharding import PartitionSpec as P

D = 8192
FB = 256
TB = 128
K = 8
LB = 11


norm_eps = 1e-06
sparsity_weight = 0.2
GRAIN = 16
VMEM = 24 * 2**20
DEPTH = 6

f32 = jnp.float32
bf16 = jnp.bfloat16


def swap(value, axis, mask):
    size = lax.axis_size(axis)
    return lax.ppermute(value, axis, [(i, i ^ mask) for i in range(size)])


def full(shape):
    return pl.BlockSpec(shape, lambda *_: (0,) * len(shape), pipeline_mode=pl.Buffered(1))


def like(shape, dtype=bf16):
    return jax.ShapeDtypeStruct(tuple(shape), dtype)


def far_memory(value):
    return pltpu.with_memory_space_constraint(value, pltpu.HBM)


def near_memory(value):
    return pltpu.with_memory_space_constraint(value, pltpu.VMEM)


class Plan:
    def __init__(self, groups, toks, rows, columns):
        self.groups, self.toks, self.rows, self.columns = groups, toks, rows, columns
        self.chips = groups // 2
        self.line = toks // 2
        self.blocks = rows // TB
        self.cap = (3 * self.blocks * K + 2 * groups - 1) // (2 * groups)
        unit = max(2, toks * GRAIN // TB)
        self.slots = -(-2 * self.cap // unit) * unit
        self.half = self.slots // 2
        self.shard = self.slots * TB // toks
        self.block = self.slots
        self.live = 2 * self.slots
        self.pair = 3 * self.slots
        self.place = self.pair + 1
        self.size = self.pair + 2
        self.every = self.chips * self.slots
        self.start = 2 * self.every
        self.cursor = self.start + LB + 1
        self.pair_all = self.cursor + LB
        self.place_all = self.pair_all + 1
        self.size_all = self.pair_all + 2
        self.trail = []

    def pin(self, value):
        return lax.optimization_barrier((value, self.trail))[0]

    def launch(
        self, kernel, name, grid, tab, ins, outs, scratch=(), into=None
    ):
        arrays, specs = [pltpu.with_memory_space_constraint(tab, pltpu.SMEM)], []
        for value, spec in ins:
            arrays.append(value)
            specs.append(full(value.shape) if spec is None else spec)
        extra = list(self.trail) if into is None else [into, *self.trail]
        count = len(specs)

        def body(tab, *refs):
            kernel(tab, *refs[:count], *refs[count + len(extra) :])

        made = pl.pallas_call(
            body,
            grid_spec=pltpu.PrefetchScalarGridSpec(
                num_scalar_prefetch=1,
                grid=grid,
                in_specs=specs + [pl.BlockSpec(memory_space=pl.ANY)] * len(extra),
                out_specs=[full(shape.shape) if spec is None else spec for shape, spec in outs],
                scratch_shapes=list(scratch),
            ),
            out_shape=[shape for shape, _ in outs],
            input_output_aliases={} if into is None else {count + 1: 0},
            compiler_params=pltpu.CompilerParams(vmem_limit_bytes=VMEM),
            cost_estimate=pl.CostEstimate(flops=1, bytes_accessed=1, transcendentals=0),
            name=name,
        )(*arrays, *extra)
        self.trail = [made[-1]]
        return made


def table_kernel(plan, ids_near, ids_far, tab):
    feat, tok = lax.axis_index("feat"), lax.axis_index("tok")
    tab[plan.pair] = tok % 2
    tab[plan.place] = tok // 2
    last = jnp.int32(0)
    for core, ids in enumerate((ids_near, ids_far)):
        base = core * plan.cap

        def entry(i, carry):
            used, last = carry
            name = ids[i // K, i % K]
            hit = (name >= feat * LB) & (name < feat * LB + LB)
            local = jnp.where(hit, name - feat * LB, last)

            @pl.when(hit)
            def _():
                tab[base + used] = core * plan.blocks + i // K
                tab[plan.block + base + used] = local
                tab[plan.live + base + used] = 1

            return used + hit.astype(jnp.int32), local

        used, last = lax.fori_loop(0, plan.blocks * K, entry, (jnp.int32(0), last))

        def empty(i, last):
            tab[base + i] = core * plan.blocks
            tab[plan.block + base + i] = last
            tab[plan.live + base + i] = 0
            return last

        lax.fori_loop(used, plan.cap if core == 0 else plan.slots - plan.cap, empty, last)


def slot_table(plan, ids):
    smem = pl.BlockSpec(memory_space=pltpu.SMEM)
    tab = pl.pallas_call(
        functools.partial(table_kernel, plan),
        out_shape=pltpu.SMEM((plan.size,), jnp.int32),
        in_specs=[smem] * 2,
        out_specs=smem,
        name="slot_table",
    )(*ids)
    plan.trail = [tab]
    return tab


def order_kernel(plan, *refs):
    tabs, every = refs[:-1], refs[-1]
    every[plan.pair_all] = tabs[0][plan.pair]
    every[plan.place_all] = tabs[0][plan.place]
    for i in range(LB + 1):
        every[plan.start + i] = 0
    for tab in tabs:

        def count(i, carry):
            at = plan.start + tab[plan.block + i] + 1
            every[at] = every[at] + tab[plan.live + i]
            return carry

        lax.fori_loop(0, plan.slots, count, 0)
    for i in range(LB):
        every[plan.start + i + 1] = every[plan.start + i] + every[plan.start + i + 1]
        every[plan.cursor + i] = every[plan.start + i]
    for chunk, tab in enumerate(tabs):

        def put(i, carry):
            @pl.when(tab[plan.live + i] > 0)
            def _():
                block = tab[plan.block + i]
                at = every[plan.cursor + block]
                every[at] = chunk * plan.slots + i
                every[plan.every + at] = chunk * 2 * plan.blocks + tab[i]
                every[plan.cursor + block] = at + 1

            return carry

        lax.fori_loop(0, plan.slots, put, 0)


def order_table(plan, tabs):
    smem = pl.BlockSpec(memory_space=pltpu.SMEM)
    every = pl.pallas_call(
        functools.partial(order_kernel, plan),
        out_shape=pltpu.SMEM((plan.size_all,), jnp.int32),
        in_specs=[smem] * len(tabs),
        out_specs=smem,
        name="order_table",
    )(*[plan.pin(tab) for tab in tabs])
    plan.trail = [every]
    return every


def block_copy(tab, at, weight, decoder, held, sems, i):
    rows = pl.ds(pl.multiple_of(tab[at] * FB, FB), FB)
    source = weight.at[rows, :] if decoder else weight.at[:, rows]
    return pltpu.make_async_copy(source, held.at[i], sems.at[i])


def half_loop(plan, own, decoder, tab, rows, weight, outs, held, sems):
    base = (tab[plan.pair] if own else 1 - tab[plan.pair]) * plan.half

    def copy(i):
        return block_copy(tab, plan.block + base + i, weight, decoder, held, sems, i)

    def start(i, carry):
        @pl.when(tab[plan.live + base + i] > 0)
        def _():
            copy(i).start()

        return carry

    def multiply(out, first, i, carry):
        live = tab[plan.live + base + i] > 0
        token = tab[base + i]
        to = pl.ds(pl.multiple_of((i - first) * TB, TB), TB)

        @pl.when(live)
        def _():
            copy(i).wait()
            at = pl.ds(pl.multiple_of(token * TB, TB), TB)
            out[to, :] = lax.dot_general(
                rows[at, :],
                held[i],
                (((1,), (1 if decoder else 0,)), ((), ())),
                preferred_element_type=f32,
            ).astype(out.dtype)

        @pl.when(jnp.logical_not(live))
        def _():
            out[to, :] = jnp.zeros((TB, FB), out.dtype)

        return carry

    def start_all():
        lax.fori_loop(0, plan.half, start, 0)

    def multiply_all():
        size = plan.half // len(outs)
        for piece, out in enumerate(outs):
            step = functools.partial(multiply, out, piece * size)
            lax.fori_loop(piece * size, (piece + 1) * size, step, 0)

    return start_all, multiply_all


def hbm():
    return pl.BlockSpec(memory_space=pltpu.HBM)


def half_scratch(plan, decoder):
    shape = (FB, plan.columns) if decoder else (plan.columns, FB)
    return [pltpu.VMEM((plan.half, *shape), bf16), pltpu.SemaphoreType.DMA((plan.half,))]


def preact_kernel(plan, own, tab, near, far, weight, *refs):
    outs, (rows, held, row_sems, sems) = refs[:-4], refs[-4:]
    moves = [
        pltpu.make_async_copy(ref, rows.at[pl.ds(i * plan.rows, plan.rows)], row_sems.at[i])
        for i, ref in enumerate((near, far))
    ]
    for move in moves:
        move.start()
    start, multiply = half_loop(plan, own, False, tab, rows, weight, outs, held, sems)
    start()
    for move in moves:
        move.wait()
    multiply()


def halves(plan, dtype, count):
    return [(like((plan.half * TB // count, FB), dtype), None)] * count


def preact_half(plan, own, tab, near, far, weight, count):
    held, sems = half_scratch(plan, False)
    return plan.launch(
        functools.partial(preact_kernel, plan, own),
        "preact_half",
        (1,),
        tab,
        [(near, hbm()), (far, hbm()), (weight, hbm())],
        halves(plan, f32 if own else bf16, count),
        [
            pltpu.VMEM((2 * plan.rows, plan.columns), bf16),
            held,
            pltpu.SemaphoreType.DMA((2,)),
            sems,
        ],
    )


def act_send_kernel(plan, count, tab, weight, near, *refs):
    parts, errs, outs = refs[:count], refs[count], refs[count + 1 : -2]
    start, multiply = half_loop(plan, False, True, tab, errs, weight, outs, *refs[-2:])
    start()
    errs[: plan.rows, :] = near[...]
    size = plan.rows // len(parts)
    for i, part in enumerate(parts):
        errs[plan.rows + i * size : plan.rows + (i + 1) * size, :] = part[...]
    multiply()


def chunk_rows(plan, chunk):
    return pl.BlockSpec(
        (2 * plan.rows, plan.columns), lambda *_: (chunk, 0), pipeline_mode=pl.Buffered(1)
    )


def act_send(plan, chunk, tab, near, parts, weight, errs, count):
    return plan.launch(
        functools.partial(act_send_kernel, plan, len(parts)),
        "act_grad_send",
        (1,),
        tab,
        [(weight, hbm()), (near, None)] + [(part, None) for part in parts],
        [
            (like((plan.chips * 2 * plan.rows, plan.columns)), chunk_rows(plan, chunk)),
            *halves(plan, bf16, count),
        ],
        half_scratch(plan, True),
        into=errs,
    )


def act_keep_kernel(plan, tab, weight, errs, out, held, sems):
    start, multiply = half_loop(plan, True, True, tab, errs, weight, [out], held, sems)
    start()
    multiply()


def act_keep(plan, chunk, tab, errs, weight):
    return plan.launch(
        functools.partial(act_keep_kernel, plan),
        "act_grad_keep",
        (1,),
        tab,
        [(weight, hbm()), (errs, chunk_rows(plan, chunk))],
        halves(plan, f32, 1),
        half_scratch(plan, True),
    )[0]


def pair_sum_kernel(plan, count, tab, keep, *refs):
    recvs, outs = refs[:count], refs[count:]
    size = plan.line // count
    for i, out in enumerate(outs):
        place = tab[plan.place] ^ i
        rows = pl.ds(pl.multiple_of(place * plan.shard, GRAIN), plan.shard)
        for piece, recv in enumerate(recvs):

            @pl.when(place // size == piece)
            def _():
                at = pl.multiple_of((place % size) * plan.shard, GRAIN)
                there = recv[pl.ds(at, plan.shard), :].astype(f32)
                out[...] = (keep[rows, :] + there).astype(out.dtype)


def pair_sum(plan, tab, keep, recvs):
    shape = (plan.shard, FB)
    return plan.launch(
        functools.partial(pair_sum_kernel, plan, len(recvs)),
        "pair_sum",
        (1,),
        tab,
        [(keep, None)] + [(recv, None) for recv in recvs],
        [(like(shape, bf16 if i else f32), None) for i in range(plan.line)],
    )


def grain_slot(plan, tab, grain):
    shard = tab[plan.pair] * plan.line + tab[plan.place]
    slot = (shard * plan.shard + grain * GRAIN) // TB
    return tab[plan.block + slot], tab[plan.live + slot] > 0


def act_kernel(plan, tab, bias, *refs):
    parts, (acts, positives) = refs[:-2], refs[-2:]
    for grain in range(plan.shard // GRAIN):
        block, live = grain_slot(plan, tab, grain)
        rows = slice(grain * GRAIN, (grain + 1) * GRAIN)
        total = bias[pl.ds(block, 1), :]
        for part in parts:
            total = total + part[rows, :].astype(f32)
        positive = jnp.where(live, jnp.maximum(total, 0.0), 0.0)
        positives[rows, :] = positive
        acts[rows, :] = (positive * positive).astype(bf16)


def shard_acts(plan, tab, bias, parts):
    shape = (plan.shard, FB)
    return plan.launch(
        functools.partial(act_kernel, plan),
        "shard_acts",
        (1,),
        tab,
        [(bias, None)] + [(part, None) for part in parts],
        [(like(shape), None), (pltpu.VMEM(shape, f32), None)],
    )


def grad_kernel(plan, tab, norms, positives, *refs):
    parts, out = refs[:-1], refs[-1]
    for grain in range(plan.shard // GRAIN):
        block, live = grain_slot(plan, tab, grain)
        rows = slice(grain * GRAIN, (grain + 1) * GRAIN)
        total = sparsity_weight * norms[pl.ds(block, 1), :]
        for part in parts:
            total = total + part[rows, :].astype(f32)
        out[rows, :] = jnp.where(live, total * 2.0 * positives[rows, :], 0.0).astype(bf16)


def shard_grads(plan, tab, norms, positives, parts):
    return plan.launch(
        functools.partial(grad_kernel, plan),
        "shard_grads",
        (1,),
        tab,
        [(norms, None), (near_memory(positives), None)] + [(part, None) for part in parts],
        [(like((plan.shard, FB)), None)],
    )[0]


def assemble(plan, pair, place, near, far, out, base):
    for side, ref in enumerate((near, far)):
        for i in range(plan.line):
            shard = (pair ^ side) * plan.line + (place ^ i)
            at = pl.multiple_of(base + shard * plan.shard, GRAIN)
            out[pl.ds(at, plan.shard), :] = ref[i * plan.shard : (i + 1) * plan.shard, :]


def recon_kernel(plan, tab, near, far, weight, acts, own, *refs):
    others, (total, held, sems) = refs[:-3], refs[-3:]
    depth = held.shape[0]

    def copy(i):
        return block_copy(tab, plan.block + i, weight, True, held, sems, i % depth)

    def start(i, carry):
        @pl.when(tab[plan.live + i] > 0)
        def _():
            copy(i).start()

        return carry

    def multiply(i, carry):
        @pl.when(tab[plan.live + i] > 0)
        def _():
            at = pl.ds(pl.multiple_of(tab[i] * TB, TB), TB)
            rows = pl.ds(pl.multiple_of(i * TB, TB), TB)
            copy(i).wait()
            total[at, :] += jnp.dot(acts[rows, :], held[i % depth], preferred_element_type=f32)

        @pl.when(i + depth < plan.slots)
        def _():
            start(i + depth, 0)

        return carry

    lax.fori_loop(0, depth, start, 0)
    assemble(plan, tab[plan.pair], tab[plan.place], near, far, acts, 0)
    total[...] = jnp.zeros_like(total)
    lax.fori_loop(0, plan.slots, multiply, 0)
    own[...] = total[: plan.rows, :]
    size = plan.rows // len(others)
    for i, other in enumerate(others):
        other[...] = total[plan.rows + i * size : plan.rows + (i + 1) * size, :].astype(bf16)


def recon(plan, chunk, tab, near, far, dec_weight, acts, pieces):
    depth = min(DEPTH, plan.slots)
    acts_shape = (plan.slots * TB, FB)
    piece = like((plan.rows // pieces, plan.columns))
    return plan.launch(
        functools.partial(recon_kernel, plan),
        "recon",
        (1,),
        tab,
        [(near, None), (far, None), (dec_weight, hbm())],
        [
            (
                like((plan.every * TB, FB)),
                pl.BlockSpec(acts_shape, lambda *_: (chunk, 0), pipeline_mode=pl.Buffered(1)),
            ),
            (like((plan.rows, plan.columns), f32), None),
        ]
        + [(piece, None)] * pieces,
        [
            pltpu.VMEM((2 * plan.rows, plan.columns), f32),
            pltpu.VMEM((depth, FB, plan.columns), bf16),
            pltpu.SemaphoreType.DMA((depth,)),
        ],
        into=acts,
    )


def column(row):
    return jnp.broadcast_to(row, (TB, row.shape[1])).T[:, :1]


def square_kernel(tab, weight, out, held, sems):
    depth = held.shape[0]

    def copy(i):
        rows = pl.ds(pl.multiple_of(i * FB, FB), FB)
        return pltpu.make_async_copy(weight.at[rows, :], held.at[i % depth], sems.at[i % depth])

    for i in range(depth):
        copy(i).start()

    def add(i, carry):
        copy(i).wait()
        value = held[i % depth].astype(f32)
        total = jnp.sum(value * value, axis=1, keepdims=True)
        out[pl.ds(i, 1), :] = jnp.broadcast_to(total, (FB, TB)).T[:1, :]

        @pl.when(i + depth < LB)
        def _():
            copy(i + depth).start()

        return carry

    lax.fori_loop(0, LB, add, 0)


def square_sums(plan, tab, dec_weight):
    return plan.launch(
        square_kernel,
        "square_sums",
        (1,),
        tab,
        [(dec_weight, hbm())],
        [(like((LB, FB), f32), None)],
        [pltpu.VMEM((DEPTH, FB, plan.columns), bf16), pltpu.SemaphoreType.DMA((DEPTH,))],
    )[0]


def turn_kernel(tab, near, far, out, mark):
    mark[...] = jnp.zeros_like(mark)
    rows = near.shape[0]
    out[:, :rows] = near[...].T
    out[:, rows:] = far[...].T


def turned(plan, chunk, tab, near, far, into):
    width = min(1024, plan.columns)
    block = pl.BlockSpec((plan.rows, width), lambda i, tab: (0, i))
    return plan.launch(
        turn_kernel,
        "turn_rows",
        (plan.columns // width,),
        tab,
        [(near, block), (far, block)],
        [
            (
                pltpu.HBM((plan.columns, plan.chips * 2 * plan.rows), bf16),
                pl.BlockSpec((width, 2 * plan.rows), lambda i, tab: (i, chunk)),
            ),
            (like((8, TB), f32), None),
        ],
        into=into,
    )[0]


def norm_add_kernel(tab, here, there, out):
    out[...] = here[...] + there[...]


def norm_add(plan, tab, here, there):
    return plan.launch(
        norm_add_kernel,
        "norm_add",
        (1,),
        tab,
        [(here, None), (there, None)],
        [(like(here.shape, f32), None)],
    )[0]


def norm_kernel(tab, here, there, total, inverse):
    norm = jnp.sqrt(here[...] + norm_eps)
    total[...] = norm + jnp.sqrt(there[...] + norm_eps)
    inverse[...] = 1.0 / norm


def norms(plan, tab, here, there):
    return plan.launch(
        norm_kernel,
        "norms",
        (1,),
        tab,
        [(here, None), (there, None)],
        [(like(here.shape, f32), None)] * 2,
    )


def two_slots(tab, plan, i, last):
    more = i + 1 < last
    j = jnp.where(more, i + 1, i)

    def at(value):
        return pl.ds(pl.multiple_of(value * TB, TB), TB)

    return more, at(tab[i]), at(tab[j]), at(tab[plan.every + i]), at(tab[plan.every + j])


def grad_dec_kernel(plan, base, tab, inverse, weight, acts, errs, out, mark, total, sums):
    mark[...] = jnp.zeros_like(mark)
    block = base + pl.program_id(0)
    first, last = tab[plan.start + block], tab[plan.start + block + 1]

    def load(i):
        more, here, there, token, other = two_slots(tab, plan, i, last)
        second = jnp.where(more, acts[there, :], jnp.zeros((TB, FB), bf16))
        these = jnp.concatenate([acts[here, :], second], axis=0).T
        rows = jnp.concatenate([errs[token, :], errs[other, :]], axis=0)
        count = jnp.dot(these, jnp.ones((2 * TB, TB), bf16), preferred_element_type=f32)
        return count, jnp.dot(these, rows, preferred_element_type=f32)

    def finish(count, value):
        scale = sparsity_weight * count[:, :1] * column(inverse[pl.ds(block, 1), :])
        out[...] = (value + scale * weight[...].astype(f32)).astype(bf16)

    @pl.when((last > first) & (last - first <= 2))
    def _():
        finish(*load(first))

    @pl.when(last - first > 2)
    def _():
        count, value = load(first)
        sums[...] = count
        total[...] = value

        def add(i, carry):
            count, value = load(first + 2 * i)
            sums[...] += count
            total[...] += value
            return carry

        lax.fori_loop(1, (last - first + 1) // 2, add, 0)
        finish(sums[...], total[...])

    @pl.when(first >= last)
    def _():
        out[...] = jnp.zeros(out.shape, bf16)


def grad_dec(plan, base, count, tab, inverse, dec_weight, acts, errs, into=None):
    shape = (FB, plan.columns)
    spec = pl.BlockSpec(shape, lambda i, tab: (base + i, 0))
    return plan.launch(
        functools.partial(grad_dec_kernel, plan, base),
        "grad_dec",
        (count,),
        tab,
        [(inverse, None), (dec_weight, spec), (acts, None), (errs, None)],
        [(like((LB * FB, plan.columns)), spec), (like((8, TB), f32), None)],
        [pltpu.VMEM(shape, f32), pltpu.VMEM((FB, TB), f32)],
        into=into,
    )[0]


def grad_enc_kernel(plan, tab, rows, *refs):
    grads, (out, total, every) = refs[: 2 * plan.chips], refs[2 * plan.chips :]
    block = pl.program_id(0)

    @pl.when(block == 0)
    def _():
        for chunk in range(plan.chips):
            near, far = grads[2 * chunk], grads[2 * chunk + 1]
            base = chunk * plan.slots * TB
            assemble(plan, tab[plan.pair_all], tab[plan.place_all], near, far, every, base)

    first, last = tab[plan.start + block], tab[plan.start + block + 1]

    def load(i):
        more, here, there, token, other = two_slots(tab, plan, i, last)
        second = jnp.where(more, every[there, :], jnp.zeros((TB, FB), bf16))
        right = jnp.concatenate([every[here, :], second], axis=0)
        left = jnp.concatenate([rows[:, token], rows[:, other]], axis=1)
        return jnp.dot(left, right, preferred_element_type=f32)

    @pl.when(last - first > 2)
    def _():
        total[...] = load(first)

        def add(i, carry):
            total[...] += load(first + 2 * i)
            return carry

        lax.fori_loop(1, (last - first + 1) // 2, add, 0)
        out[...] = total[...].astype(bf16)

    @pl.when((last > first) & (last - first <= 2))
    def _():
        out[...] = load(first).astype(bf16)

    @pl.when(last == first)
    def _():
        out[...] = jnp.zeros(out.shape, bf16)


def grad_enc(plan, tab, grads, rows):
    shape = (plan.columns, FB)
    return plan.launch(
        functools.partial(grad_enc_kernel, plan),
        "grad_enc",
        (LB,),
        tab,
        [(value, None) for value in (rows, *grads)],
        [(like((plan.columns, LB * FB)), pl.BlockSpec(shape, lambda i, tab: (0, i)))],
        [pltpu.VMEM(shape, f32), pltpu.VMEM((plan.every * TB, FB), bf16)],
    )[0]


def join_kernel(tab, *refs):
    out = refs[-1]
    for i, ref in enumerate(refs[:-1]):
        out[i * ref.shape[0] : (i + 1) * ref.shape[0], :] = ref[...]


def join(plan, tab, parts):
    return plan.launch(
        join_kernel,
        "join_shards",
        (1,),
        tab,
        [(part, None) for part in parts],
        [(like((plan.half * TB, FB)), None)],
    )[0]


def chip_sum_kernel(tab, own, *refs):
    others, total = refs[:-1], refs[-1]
    size = others[0].shape[0]
    for i, other in enumerate(others):
        at = slice(i * size, (i + 1) * size)
        total[at, :] = (own[at, :] + other[...].astype(f32)).astype(bf16)


def chip_sum(plan, tab, own, others):
    return plan.launch(
        chip_sum_kernel,
        "chip_sum",
        (1,),
        tab,
        [(own, None)] + [(other, None) for other in others],
        [(like(own.shape), None)],
    )[0]


def error_kernel(pieces, tab, total, bias, rows, *refs):
    others, near, parts = refs[: -1 - pieces], refs[-1 - pieces], refs[-pieces:]
    size = parts[0].shape[0]
    for i, part in enumerate(parts):
        at = slice(i * size, (i + 1) * size)
        value = total[at, :].astype(f32)
        for other in others:
            value = value + other[at, :].astype(f32)
        error = value + bias[...] - rows[at, :].astype(f32)
        error = (error * TB ** (-0.5)).astype(bf16)
        near[at, :] = error
        part[...] = error


def errors(plan, tab, total, bias, rows, received, pieces):
    piece = like((plan.rows // pieces, plan.columns))
    return plan.launch(
        functools.partial(error_kernel, pieces),
        "errors",
        (1,),
        tab,
        [(total, None), (bias, None), (rows, None)] + [(value, None) for value in received],
        [(like(rows.shape), None)] + [(piece, None)] * pieces,
    )


def spread_parts(plan, parts):
    return [parts[0]] + [swap(parts[i], "tok", 2 * i) for i in range(1, plan.line)]


def spread_shard(plan, shard):
    return [shard] + [swap(shard, "tok", 2 * i) for i in range(1, plan.line)]


def on_device(resid, enc_weight, enc_bias, dec_weight, dec_bias, active_ids, active_count):
    plan = Plan(lax.axis_size("feat"), lax.axis_size("tok"), *resid.shape)
    chips = range(plan.chips)
    rest = list(chips[1:])
    enc_weight, dec_weight = far_memory(enc_weight), far_memory(dec_weight)
    bias = enc_bias.reshape(LB, FB)
    back = dec_bias[None, :]

    def from_chip(value, chunk):
        return swap(value, "feat", 2 * chunk)

    def both(value):
        return value, swap(value, "feat", 1)

    entries = jnp.where(jnp.arange(K)[None, :] < active_count[:, None], active_ids, -1)
    lists = {chunk: from_chip(entries, chunk) for chunk in rest}
    tabs = {0: slot_table(plan, both(entries))}
    rows = {0: [far_memory(resid), near_memory(swap(resid, "feat", 1))]}
    arriving = {chunk: from_chip(resid, chunk) for chunk in rest}
    sends, keeps, parts, shards, positives, sums, received, fresh = ({} for _ in range(8))
    turns = acts = errs = None

    def send_products(chunk):
        pieces = preact_half(plan, False, tabs[chunk], *rows[chunk], enc_weight, 2 if chunk else 1)
        sends[chunk] = [swap(piece, "tok", 1) for piece in pieces]

    def keep_products(chunk):
        keeps[chunk] = preact_half(plan, True, tabs[chunk], *rows[chunk], enc_weight, 1)[0]

    def add_norms(squares, bits):
        for bit in bits:
            squares = norm_add(plan, tabs[0], squares, swap(squares, "tok", bit))
        return squares

    def reduce_pairs(chunk):
        parts[chunk] = spread_parts(plan, pair_sum(plan, tabs[chunk], keeps[chunk], sends[chunk]))

    def activate(chunk):
        shard, positives[chunk] = shard_acts(plan, tabs[chunk], bias, parts[chunk])
        shards[chunk] = spread_shard(plan, shard)

    def gather(chunk):
        near = join(plan, tabs[chunk], shards[chunk])
        shards[chunk] = (near, swap(near, "tok", 1))

    def rebuild(chunk, acts):
        acts, own, *others = recon(plan, chunk, tabs[chunk], *shards[chunk], dec_weight, acts, 4 if chunk else 1)
        sums[chunk] = (own, [swap(other, "feat", 1) for other in others])
        return acts

    def total(chunk):
        sums[chunk] = chip_sum(plan, tabs[chunk], *sums[chunk])
        for step in rest:
            received[chunk ^ step, step] = from_chip(sums[chunk], step)

    def compare(chunk):
        others = [received[chunk, step] for step in rest]
        near, *pieces = errors(plan, tabs[chunk], sums[chunk], back, rows[chunk][0], others, 4 if chunk else 1)
        fresh[chunk] = (near, [swap(piece, "feat", 1) for piece in pieces])

    def back_send(chunk, errs):
        count = 1 if chunk else 2
        errs, *pieces = act_send(plan, chunk, tabs[chunk], *fresh[chunk], dec_weight, errs, count)
        sends[chunk] = [swap(piece, "tok", 1) for piece in pieces]
        return errs

    def back_keep(chunk, errs):
        keeps[chunk] = act_keep(plan, chunk, tabs[chunk], errs, dec_weight)

    def differentiate(chunk):
        shard = shard_grads(plan, tabs[chunk], norm_sum, positives[chunk], parts[chunk])
        shards[chunk] = spread_shard(plan, shard)

    bits = [1 << i for i in range((plan.toks - 1).bit_length())]
    send_products(0)
    keep_products(0)
    reduce_pairs(0)
    for chunk in rest:
        tabs[chunk] = slot_table(plan, both(plan.pin(lists[chunk])))
        rows[chunk] = [near_memory(value) for value in both(plan.pin(arriving[chunk]))]
        send_products(chunk)
    activate(0)
    for chunk in rest:
        keep_products(chunk)
        reduce_pairs(chunk)
    gather(0)
    squares = square_sums(plan, tabs[0], dec_weight)
    for chunk in rest:
        activate(chunk)
    acts = rebuild(0, acts)
    total(0)
    for chunk in rest:
        gather(chunk)
    squares = add_norms(squares, bits[1:-1])
    order = order_table(plan, [tabs[chunk] for chunk in chips])
    for chunk in rest:
        acts = rebuild(chunk, acts)
    squares = add_norms(squares, bits[:1])
    for chunk in rest:
        total(chunk)

    for chunk in rest:
        compare(chunk)
        errs = back_send(chunk, errs)
        back_keep(chunk, errs)
    norm_sum, inverse = norms(plan, tabs[0], squares, swap(squares, "tok", bits[-1]))
    for chunk in rest:
        reduce_pairs(chunk)
    for chunk in chips:
        turns = turned(plan, chunk, tabs[chunk], *rows[chunk], turns)
    compare(0)
    errs = back_send(0, errs)
    back_keep(0, errs)
    reduce_pairs(0)
    for chunk in rest:
        differentiate(chunk)
    values = (order, inverse, dec_weight, acts, errs)
    out_dec = grad_dec(plan, 0, 4, *values)
    for chunk in rest:
        gather(chunk)
    differentiate(0)
    out_dec = grad_dec(plan, 4, 4, *values, into=out_dec)
    gather(0)
    out_dec = grad_dec(plan, 8, LB - 8, *values, into=out_dec)
    out_enc = grad_enc(plan, order, [piece for chunk in chips for piece in shards[chunk]], turns)
    return (out_enc, out_dec)


def solution(mesh):
    return jax.shard_map(
        on_device,
        mesh=mesh,
        in_specs=(
            P("feat", "tok"),
            P("tok", "feat"),
            P("feat"),
            P("feat", "tok"),
            P("tok"),
            P("feat", None),
            P("feat"),
        ),
        out_specs=(P("tok", "feat"), P("feat", "tok")),
        check_vma=False,
    )
```

```python
import functools

import jax
import jax.numpy as jnp
from jax import lax
from jax.experimental import pallas as pl
from jax.experimental.pallas import tpu as pltpu
from jax.sharding import PartitionSpec as P

D = 8192
FB = 256
TB = 128
K = 8
LB = 11


norm_eps = 1e-06
sparsity_weight = 0.2
GRAIN = 16
VMEM = 24 * 2**20
DEPTH = 6

f32 = jnp.float32
bf16 = jnp.bfloat16


def swap(value, axis, mask):
    size = lax.axis_size(axis)
    return lax.ppermute(value, axis, [(i, i ^ mask) for i in range(size)])


def full(shape):
    return pl.BlockSpec(shape, lambda *_: (0,) * len(shape), pipeline_mode=pl.Buffered(1))


def like(shape, dtype=bf16):
    return jax.ShapeDtypeStruct(tuple(shape), dtype)


def far_memory(value):
    return pltpu.with_memory_space_constraint(value, pltpu.HBM)


def near_memory(value):
    return pltpu.with_memory_space_constraint(value, pltpu.VMEM)


class Plan:
    def __init__(self, groups, toks, rows, columns):
        self.groups, self.toks, self.rows, self.columns = groups, toks, rows, columns
        self.chips = groups // 2
        self.line = toks // 2
        self.blocks = rows // TB
        self.cap = (3 * self.blocks * K + 2 * groups - 1) // (2 * groups)
        unit = max(2, toks * GRAIN // TB)
        self.slots = -(-2 * self.cap // unit) * unit
        self.half = self.slots // 2
        self.shard = self.slots * TB // toks
        self.block = self.slots
        self.live = 2 * self.slots
        self.pair = 3 * self.slots
        self.place = self.pair + 1
        self.size = self.pair + 2
        self.every = self.chips * self.slots
        self.start = 2 * self.every
        self.cursor = self.start + LB + 1
        self.pair_all = self.cursor + LB
        self.place_all = self.pair_all + 1
        self.size_all = self.pair_all + 2
        self.trail = []

    def pin(self, value):
        return lax.optimization_barrier((value, self.trail))[0]

    def launch(
        self, kernel, name, grid, tab, ins, outs, scratch=(), into=None, after=()
    ):
        arrays, specs = [pltpu.with_memory_space_constraint(tab, pltpu.SMEM)], []
        for value, spec in ins:
            arrays.append(value)
            specs.append(full(value.shape) if spec is None else spec)
        extra = [*([] if into is None else [into]), *self.trail, *after]
        count = len(specs)

        def body(tab, *refs):
            kernel(tab, *refs[:count], *refs[count + len(extra) :])

        made = pl.pallas_call(
            body,
            grid_spec=pltpu.PrefetchScalarGridSpec(
                num_scalar_prefetch=1,
                grid=grid,
                in_specs=specs + [pl.BlockSpec(memory_space=pl.ANY)] * len(extra),
                out_specs=[full(shape.shape) if spec is None else spec for shape, spec in outs],
                scratch_shapes=list(scratch),
            ),
            out_shape=[shape for shape, _ in outs],
            input_output_aliases={} if into is None else {count + 1: 0},
            compiler_params=pltpu.CompilerParams(vmem_limit_bytes=VMEM),
            cost_estimate=pl.CostEstimate(flops=1, bytes_accessed=1, transcendentals=0),
            name=name,
        )(*arrays, *extra)
        self.trail = [made[-1]]
        return made


def table_kernel(plan, ids_near, ids_far, *refs):
    tab = refs[-1]
    feat, tok = lax.axis_index("feat"), lax.axis_index("tok")
    tab[plan.pair] = tok % 2
    tab[plan.place] = tok // 2
    last = jnp.int32(0)
    for core, ids in enumerate((ids_near, ids_far)):
        base = core * plan.half

        def entry(i, carry):
            used, last = carry
            name = ids[i // K, i % K]
            hit = (name >= feat * LB) & (name < feat * LB + LB)
            local = jnp.where(hit, name - feat * LB, last)

            @pl.when(hit)
            def _():
                tab[base + used] = core * plan.blocks + i // K
                tab[plan.block + base + used] = local
                tab[plan.live + base + used] = 1

            return used + hit.astype(jnp.int32), local

        used, last = lax.fori_loop(0, plan.blocks * K, entry, (jnp.int32(0), last))

        def empty(i, last):
            tab[base + i] = core * plan.blocks
            tab[plan.block + base + i] = last
            tab[plan.live + base + i] = 0
            return last

        lax.fori_loop(used, plan.half, empty, last)


def slot_table(plan, ids):
    smem = pl.BlockSpec(memory_space=pltpu.SMEM)
    tab = pl.pallas_call(
        functools.partial(table_kernel, plan),
        out_shape=pltpu.SMEM((plan.size,), jnp.int32),
        in_specs=[smem] * 2 + [pl.BlockSpec(memory_space=pl.ANY)] * len(plan.trail),
        out_specs=smem,
        name="slot_table",
    )(*ids, *plan.trail)
    plan.trail = [tab]
    return tab


def order_kernel(plan, *refs):
    tabs, every = refs[:-1], refs[-1]
    every[plan.pair_all] = tabs[0][plan.pair]
    every[plan.place_all] = tabs[0][plan.place]
    for i in range(LB + 1):
        every[plan.start + i] = 0
    for tab in tabs:

        def count(i, carry):
            at = plan.start + tab[plan.block + i] + 1
            every[at] = every[at] + tab[plan.live + i]
            return carry

        lax.fori_loop(0, plan.slots, count, 0)
    for i in range(LB):
        every[plan.start + i + 1] = every[plan.start + i] + every[plan.start + i + 1]
        every[plan.cursor + i] = every[plan.start + i]
    for chunk, tab in enumerate(tabs):

        def put(i, carry):
            @pl.when(tab[plan.live + i] > 0)
            def _():
                block = tab[plan.block + i]
                at = every[plan.cursor + block]
                every[at] = chunk * plan.slots + i
                every[plan.every + at] = chunk * 2 * plan.blocks + tab[i]
                every[plan.cursor + block] = at + 1

            return carry

        lax.fori_loop(0, plan.slots, put, 0)


def order_table(plan, tabs):
    smem = pl.BlockSpec(memory_space=pltpu.SMEM)
    every = pl.pallas_call(
        functools.partial(order_kernel, plan),
        out_shape=pltpu.SMEM((plan.size_all,), jnp.int32),
        in_specs=[smem] * len(tabs),
        out_specs=smem,
        name="order_table",
    )(*[plan.pin(tab) for tab in tabs])
    plan.trail = [every]
    return every


def block_copy(tab, at, weight, decoder, held, sems, i):
    rows = pl.ds(pl.multiple_of(tab[at] * FB, FB), FB)
    source = weight.at[rows, :] if decoder else weight.at[:, rows]
    return pltpu.make_async_copy(source, held.at[i], sems.at[i])


def half_loop(plan, own, decoder, tab, rows, base_row, weight, outs, held, sems):
    base = (tab[plan.pair] if own else 1 - tab[plan.pair]) * plan.half

    def copy(i):
        return block_copy(tab, plan.block + base + i, weight, decoder, held, sems, i)

    def start(i, carry):
        @pl.when(tab[plan.live + base + i] > 0)
        def _():
            copy(i).start()

        return carry

    def multiply(out, first, i, carry):
        live = tab[plan.live + base + i] > 0
        token = tab[base + i]
        to = pl.ds(pl.multiple_of((i - first) * TB, TB), TB)

        @pl.when(live)
        def _():
            copy(i).wait()
            at = pl.ds(pl.multiple_of((token - base_row) * TB, TB), TB)
            out[to, :] = lax.dot_general(
                rows[at, :],
                held[i],
                (((1,), (1 if decoder else 0,)), ((), ())),
                preferred_element_type=f32,
            ).astype(out.dtype)

        @pl.when(jnp.logical_not(live))
        def _():
            out[to, :] = jnp.zeros((TB, FB), out.dtype)

        return carry

    def start_all():
        lax.fori_loop(0, plan.half, start, 0)

    def multiply_all():
        size = plan.half // len(outs)
        for piece, out in enumerate(outs):
            step = functools.partial(multiply, out, piece * size)
            lax.fori_loop(piece * size, (piece + 1) * size, step, 0)

    return start_all, multiply_all


def hbm():
    return pl.BlockSpec(memory_space=pltpu.HBM)


def half_scratch(plan, decoder):
    shape = (FB, plan.columns) if decoder else (plan.columns, FB)
    return [pltpu.VMEM((plan.half, *shape), bf16), pltpu.SemaphoreType.DMA((plan.half,))]


def preact_kernel(plan, own, tab, near, far, weight, *refs):
    outs, (rows, held, row_sem, sems) = refs[:-4], refs[-4:]
    home = tab[plan.pair] if own else 1 - tab[plan.pair]
    moves = [pltpu.make_async_copy(ref, rows, row_sem) for ref in (near, far)]
    for core, move in enumerate(moves):
        pl.when(home == core)(move.start)
    base_row = home * plan.blocks
    start, multiply = half_loop(plan, own, False, tab, rows, base_row, weight, outs, held, sems)
    start()
    moves[0].wait()
    multiply()


def halves(plan, dtype, count):
    return [(like((plan.half * TB // count, FB), dtype), None)] * count


def preact_half(plan, own, tab, near, far, weight, count):
    held, sems = half_scratch(plan, False)
    return plan.launch(
        functools.partial(preact_kernel, plan, own),
        "preact_half",
        (1,),
        tab,
        [(near, hbm()), (far, hbm()), (weight, hbm())],
        halves(plan, f32 if own else bf16, count),
        [
            pltpu.VMEM((plan.rows, plan.columns), bf16),
            held,
            pltpu.SemaphoreType.DMA,
            sems,
        ],
    )


def act_send_kernel(plan, tab, weight, near, *refs):
    base_row = (1 - tab[plan.pair]) * plan.blocks
    outs, (held, sems) = refs[:-2], refs[-2:]
    start, multiply = half_loop(plan, False, True, tab, near, base_row, weight, outs, held, sems)
    start()
    multiply()


def chunk_rows(plan, chunk):
    return pl.BlockSpec(
        (2 * plan.rows, plan.columns), lambda *_: (chunk, 0), pipeline_mode=pl.Buffered(1)
    )


def act_send(plan, tab, near, weight, after):
    return plan.launch(
        functools.partial(act_send_kernel, plan),
        "act_grad_send",
        (1,),
        tab,
        [(weight, hbm()), (near, None)],
        halves(plan, bf16, 1),
        half_scratch(plan, True),
        after=after,
    )[0]


def act_keep_kernel(plan, count, tab, weight, near, *refs):
    parts, errs, outs = refs[:count], refs[count], refs[count + 1 : -2]
    start, multiply = half_loop(plan, True, True, tab, errs, 0, weight, outs, *refs[-2:])
    start()
    here = pl.multiple_of((1 - tab[plan.pair]) * plan.rows, TB)
    errs[pl.ds(here, plan.rows), :] = near[...]
    size = plan.rows // count
    for i, part in enumerate(parts):
        there = pl.multiple_of(tab[plan.pair] * plan.rows + i * size, GRAIN)
        errs[pl.ds(there, size), :] = part[...]
    multiply()


def act_keep(plan, chunk, tab, near, parts, weight, errs):
    return plan.launch(
        functools.partial(act_keep_kernel, plan, len(parts)),
        "act_grad_keep",
        (1,),
        tab,
        [(weight, hbm()), (near, None)] + [(part, None) for part in parts],
        [
            (like((plan.chips * 2 * plan.rows, plan.columns)), chunk_rows(plan, chunk)),
            *halves(plan, f32, 1),
        ],
        half_scratch(plan, True),
        into=errs,
    )


def pair_sum_kernel(plan, count, tab, keep, *refs):
    recvs, outs = refs[:count], refs[count:]
    size = plan.line // count
    for i, out in enumerate(outs):
        place = tab[plan.place] ^ i
        rows = pl.ds(pl.multiple_of(place * plan.shard, GRAIN), plan.shard)
        for piece, recv in enumerate(recvs):

            @pl.when(place // size == piece)
            def _():
                at = pl.multiple_of((place % size) * plan.shard, GRAIN)
                there = recv[pl.ds(at, plan.shard), :].astype(f32)
                out[...] = (keep[rows, :] + there).astype(out.dtype)


def pair_sum(plan, tab, keep, recvs):
    shape = (plan.shard, FB)
    return plan.launch(
        functools.partial(pair_sum_kernel, plan, len(recvs)),
        "pair_sum",
        (1,),
        tab,
        [(keep, None)] + [(recv, None) for recv in recvs],
        [(like(shape, bf16 if i else f32), None) for i in range(plan.line)],
    )


def grain_slot(plan, tab, grain):
    shard = tab[plan.pair] * plan.line + tab[plan.place]
    slot = (shard * plan.shard + grain * GRAIN) // TB
    return tab[plan.block + slot], tab[plan.live + slot] > 0


def act_kernel(plan, tab, bias, *refs):
    parts, (acts, positives) = refs[:-2], refs[-2:]
    for grain in range(plan.shard // GRAIN):
        block, live = grain_slot(plan, tab, grain)
        rows = slice(grain * GRAIN, (grain + 1) * GRAIN)
        total = bias[pl.ds(block, 1), :]
        for part in parts:
            total = total + part[rows, :].astype(f32)
        positive = jnp.where(live, jnp.maximum(total, 0.0), 0.0)
        positives[rows, :] = positive
        acts[rows, :] = (positive * positive).astype(bf16)


def shard_acts(plan, tab, bias, parts):
    shape = (plan.shard, FB)
    return plan.launch(
        functools.partial(act_kernel, plan),
        "shard_acts",
        (1,),
        tab,
        [(bias, None)] + [(part, None) for part in parts],
        [(like(shape), None), (pltpu.VMEM(shape, f32), None)],
    )


def grad_kernel(plan, tab, norms, positives, *refs):
    parts, out = refs[:-1], refs[-1]
    for grain in range(plan.shard // GRAIN):
        block, live = grain_slot(plan, tab, grain)
        rows = slice(grain * GRAIN, (grain + 1) * GRAIN)
        total = sparsity_weight * norms[pl.ds(block, 1), :]
        for part in parts:
            total = total + part[rows, :].astype(f32)
        out[rows, :] = jnp.where(live, total * 2.0 * positives[rows, :], 0.0).astype(bf16)


def shard_grads(plan, tab, norms, positives, parts):
    return plan.launch(
        functools.partial(grad_kernel, plan),
        "shard_grads",
        (1,),
        tab,
        [(norms, None), (near_memory(positives), None)] + [(part, None) for part in parts],
        [(like((plan.shard, FB)), None)],
    )[0]


def assemble(plan, pair, place, near, far, out, base):
    for side, refs in enumerate((near, far)):
        size = plan.line // len(refs)
        for i in range(plan.line):
            shard = (pair ^ side) * plan.line + (place ^ i)
            at = pl.multiple_of(base + shard * plan.shard, GRAIN)
            part = slice(i % size * plan.shard, (i % size + 1) * plan.shard)
            out[pl.ds(at, plan.shard), :] = refs[i // size][part, :]


def recon_kernel(plan, count, tab, *refs):
    near, far = refs[:count], refs[count : 2 * count]
    weight, acts, total, *refs = refs[2 * count :]
    others, (held, sems) = refs[:-2], refs[-2:]
    depth = held.shape[0]

    def copy(i):
        return block_copy(tab, plan.block + i, weight, True, held, sems, i % depth)

    def start(i, carry):
        @pl.when(tab[plan.live + i] > 0)
        def _():
            copy(i).start()

        return carry

    def multiply(i, carry):
        @pl.when(tab[plan.live + i] > 0)
        def _():
            at = pl.ds(pl.multiple_of(tab[i] * TB, TB), TB)
            rows = pl.ds(pl.multiple_of(i * TB, TB), TB)
            copy(i).wait()
            total[at, :] += jnp.dot(acts[rows, :], held[i % depth], preferred_element_type=f32)

        @pl.when(i + depth < plan.slots)
        def _():
            start(i + depth, 0)

        return carry

    lax.fori_loop(0, depth, start, 0)
    assemble(plan, tab[plan.pair], tab[plan.place], near, far, acts, 0)
    total[...] = jnp.zeros_like(total)
    lax.fori_loop(0, plan.slots, multiply, 0)
    size = plan.rows // len(others)
    for i, other in enumerate(others):
        at = pl.multiple_of(tab[plan.pair] * plan.rows + i * size, GRAIN)
        other[...] = total[pl.ds(at, size), :].astype(bf16)


def recon(plan, chunk, tab, near, far, dec_weight, acts, pieces):
    depth = min(DEPTH, plan.slots)
    acts_shape = (plan.slots * TB, FB)
    piece = like((plan.rows // pieces, plan.columns))
    return plan.launch(
        functools.partial(recon_kernel, plan, len(near)),
        "recon",
        (1,),
        tab,
        [(value, None) for value in (*near, *far)] + [(dec_weight, hbm())],
        [
            (
                like((plan.every * TB, FB)),
                pl.BlockSpec(acts_shape, lambda *_: (chunk, 0), pipeline_mode=pl.Buffered(1)),
            ),
            (like((2 * plan.rows, plan.columns), f32), None),
        ]
        + [(piece, None)] * pieces,
        [
            pltpu.VMEM((depth, FB, plan.columns), bf16),
            pltpu.SemaphoreType.DMA((depth,)),
        ],
        into=acts,
    )


def column(row):
    return jnp.broadcast_to(row, (TB, row.shape[1])).T[:, :1]


def square_kernel(tab, weight, out, held, sems):
    depth = held.shape[0]

    def copy(i):
        rows = pl.ds(pl.multiple_of(i * FB, FB), FB)
        return pltpu.make_async_copy(weight.at[rows, :], held.at[i % depth], sems.at[i % depth])

    for i in range(depth):
        copy(i).start()

    def add(i, carry):
        copy(i).wait()
        value = held[i % depth].astype(f32)
        total = jnp.sum(value * value, axis=1, keepdims=True)
        out[pl.ds(i, 1), :] = jnp.broadcast_to(total, (FB, TB)).T[:1, :]

        @pl.when(i + depth < LB)
        def _():
            copy(i + depth).start()

        return carry

    lax.fori_loop(0, LB, add, 0)


def square_sums(plan, tab, dec_weight):
    return plan.launch(
        square_kernel,
        "square_sums",
        (1,),
        tab,
        [(dec_weight, hbm())],
        [(like((LB, FB), f32), None)],
        [pltpu.VMEM((DEPTH, FB, plan.columns), bf16), pltpu.SemaphoreType.DMA((DEPTH,))],
    )[0]


def turn_kernel(tab, near, far, out, mark):
    mark[...] = jnp.zeros_like(mark)
    rows = near.shape[0]
    out[:, :rows] = near[...].T
    out[:, rows:] = far[...].T


def turned(plan, chunk, tab, near, far, into):
    width = min(1024, plan.columns)
    block = pl.BlockSpec((plan.rows, width), lambda i, tab: (0, i))
    return plan.launch(
        turn_kernel,
        "turn_rows",
        (plan.columns // width,),
        tab,
        [(near, block), (far, block)],
        [
            (
                pltpu.HBM((plan.columns, plan.chips * 2 * plan.rows), bf16),
                pl.BlockSpec((width, 2 * plan.rows), lambda i, tab: (i, chunk)),
            ),
            (like((8, TB), f32), None),
        ],
        into=into,
    )[0]


def norm_add_kernel(tab, here, there, out):
    out[...] = here[...] + there[...]


def norm_add(plan, tab, here, there):
    return plan.launch(
        norm_add_kernel,
        "norm_add",
        (1,),
        tab,
        [(here, None), (there, None)],
        [(like(here.shape, f32), None)],
    )[0]


def norm_kernel(tab, here, there, total, inverse):
    norm = jnp.sqrt(here[...] + norm_eps)
    total[...] = norm + jnp.sqrt(there[...] + norm_eps)
    inverse[...] = 1.0 / norm


def norms(plan, tab, here, there):
    return plan.launch(
        norm_kernel,
        "norms",
        (1,),
        tab,
        [(here, None), (there, None)],
        [(like(here.shape, f32), None)] * 2,
    )


def two_slots(tab, plan, i, last):
    more = i + 1 < last
    j = jnp.where(more, i + 1, i)

    def at(value):
        return pl.ds(pl.multiple_of(value * TB, TB), TB)

    return more, at(tab[i]), at(tab[j]), at(tab[plan.every + i]), at(tab[plan.every + j])


def grad_dec_kernel(plan, base, tab, inverse, weight, acts, errs, out, mark, total, sums):
    mark[...] = jnp.zeros_like(mark)
    block = base + pl.program_id(0)
    first, last = tab[plan.start + block], tab[plan.start + block + 1]

    def load(i):
        more, here, there, token, other = two_slots(tab, plan, i, last)
        second = jnp.where(more, acts[there, :], jnp.zeros((TB, FB), bf16))
        these = jnp.concatenate([acts[here, :], second], axis=0).T
        rows = jnp.concatenate([errs[token, :], errs[other, :]], axis=0)
        count = jnp.dot(these, jnp.ones((2 * TB, TB), bf16), preferred_element_type=f32)
        return count, jnp.dot(these, rows, preferred_element_type=f32)

    def finish(count, value):
        scale = sparsity_weight * count[:, :1] * column(inverse[pl.ds(block, 1), :])
        out[...] = (value + scale * weight[...].astype(f32)).astype(bf16)

    @pl.when((last > first) & (last - first <= 2))
    def _():
        finish(*load(first))

    @pl.when(last - first > 2)
    def _():
        count, value = load(first)
        sums[...] = count
        total[...] = value

        def add(i, carry):
            count, value = load(first + 2 * i)
            sums[...] += count
            total[...] += value
            return carry

        lax.fori_loop(1, (last - first + 1) // 2, add, 0)
        finish(sums[...], total[...])

    @pl.when(first >= last)
    def _():
        out[...] = jnp.zeros(out.shape, bf16)


def grad_dec(plan, base, count, tab, inverse, dec_weight, acts, errs, into=None):
    shape = (FB, plan.columns)
    spec = pl.BlockSpec(shape, lambda i, tab: (base + i, 0))
    return plan.launch(
        functools.partial(grad_dec_kernel, plan, base),
        "grad_dec",
        (count,),
        tab,
        [(inverse, None), (dec_weight, spec), (acts, None), (errs, None)],
        [(like((LB * FB, plan.columns)), spec), (like((8, TB), f32), None)],
        [pltpu.VMEM(shape, f32), pltpu.VMEM((FB, TB), f32)],
        into=into,
    )[0]


def grad_enc_kernel(plan, tab, rows, *refs):
    grads, (out, total, every) = refs[: 2 * plan.chips], refs[2 * plan.chips :]
    block = pl.program_id(0)

    @pl.when(block == 0)
    def _():
        for chunk in range(plan.chips):
            near, far = grads[2 * chunk], grads[2 * chunk + 1]
            base = chunk * plan.slots * TB
            assemble(plan, tab[plan.pair_all], tab[plan.place_all], [near], [far], every, base)

    first, last = tab[plan.start + block], tab[plan.start + block + 1]

    def load(i):
        more, here, there, token, other = two_slots(tab, plan, i, last)
        second = jnp.where(more, every[there, :], jnp.zeros((TB, FB), bf16))
        right = jnp.concatenate([every[here, :], second], axis=0)
        left = jnp.concatenate([rows[:, token], rows[:, other]], axis=1)
        return jnp.dot(left, right, preferred_element_type=f32)

    @pl.when(last - first > 2)
    def _():
        total[...] = load(first)

        def add(i, carry):
            total[...] += load(first + 2 * i)
            return carry

        lax.fori_loop(1, (last - first + 1) // 2, add, 0)
        out[...] = total[...].astype(bf16)

    @pl.when((last > first) & (last - first <= 2))
    def _():
        out[...] = load(first).astype(bf16)

    @pl.when(last == first)
    def _():
        out[...] = jnp.zeros(out.shape, bf16)


def grad_enc(plan, tab, grads, rows):
    shape = (plan.columns, FB)
    return plan.launch(
        functools.partial(grad_enc_kernel, plan),
        "grad_enc",
        (LB,),
        tab,
        [(value, None) for value in (rows, *grads)],
        [(like((plan.columns, LB * FB)), pl.BlockSpec(shape, lambda i, tab: (0, i)))],
        [pltpu.VMEM(shape, f32), pltpu.VMEM((plan.every * TB, FB), bf16)],
    )[0]


def join_kernel(plan, tab, *refs):
    parts, outs = refs[: plan.line], refs[plan.line :]
    size = plan.line // len(outs)
    for i, part in enumerate(parts):
        rows = slice(i % size * plan.shard, (i % size + 1) * plan.shard)
        outs[i // size][rows, :] = part[...]


def join(plan, tab, parts, count):
    return plan.launch(
        functools.partial(join_kernel, plan),
        "join_shards",
        (1,),
        tab,
        [(part, None) for part in parts],
        halves(plan, bf16, count),
    )


def chip_sum_kernel(plan, tab, both, *refs):
    others, total = refs[:-1], refs[-1]
    size = plan.rows // len(others)
    for i, other in enumerate(others):
        at = pl.multiple_of((1 - tab[plan.pair]) * plan.rows + i * size, GRAIN)
        value = both[pl.ds(at, size), :] + other[...].astype(f32)
        total[i * size : (i + 1) * size, :] = value.astype(bf16)


def chip_sum(plan, tab, both, others):
    return plan.launch(
        functools.partial(chip_sum_kernel, plan),
        "chip_sum",
        (1,),
        tab,
        [(both, None)] + [(other, None) for other in others],
        [(like((plan.rows, plan.columns)), None)],
    )[0]


def error_kernel(plan, pieces, tab, total, bias, near_rows, far_rows, *refs):
    others, near, parts = refs[: -1 - pieces], refs[-1 - pieces], refs[-pieces:]
    size = plan.rows // pieces
    for core, rows in enumerate((near_rows, far_rows)):

        @pl.when(1 - tab[plan.pair] == core)
        def _():
            for i, part in enumerate(parts):
                at = slice(i * size, (i + 1) * size)
                value = total[at, :].astype(f32)
                for other in others:
                    value = value + other[at, :].astype(f32)
                error = value + bias[...] - rows[at, :].astype(f32)
                error = (error * TB ** (-0.5)).astype(bf16)
                near[at, :] = error
                part[...] = error


def errors(plan, tab, total, bias, rows, received, pieces):
    piece = like((plan.rows // pieces, plan.columns))
    return plan.launch(
        functools.partial(error_kernel, plan, pieces),
        "errors",
        (1,),
        tab,
        [(value, None) for value in (total, bias, *rows, *received)],
        [(like(total.shape), None)] + [(piece, None)] * pieces,
    )


def spread_parts(plan, parts):
    return [parts[0]] + [swap(parts[i], "tok", 2 * i) for i in range(1, plan.line)]


def spread_shard(plan, shard):
    return [shard] + [swap(shard, "tok", 2 * i) for i in range(1, plan.line)]


def on_device(resid, enc_weight, enc_bias, dec_weight, dec_bias, active_ids, active_count):
    plan = Plan(lax.axis_size("feat"), lax.axis_size("tok"), *resid.shape)
    chips = range(plan.chips)
    rest = list(chips[1:])
    enc_weight, dec_weight = far_memory(enc_weight), far_memory(dec_weight)
    bias = enc_bias.reshape(LB, FB)
    back = dec_bias[None, :]

    def from_chip(value, chunk):
        return swap(value, "feat", 2 * chunk)

    def both(value):
        return value, swap(value, "feat", 1)

    entries = jnp.where(jnp.arange(K)[None, :] < active_count[:, None], active_ids, -1)
    entries, moving = lax.optimization_barrier((entries, resid))
    lists = {chunk: from_chip(entries, chunk) for chunk in rest}
    tabs = {0: slot_table(plan, both(entries))}
    rows = {0: [far_memory(resid), near_memory(swap(resid, "feat", 1))]}
    arriving = {chunk: from_chip(moving, chunk) for chunk in rest}
    sends, keeps, parts, shards, positives, sums, received, fresh = ({} for _ in range(8))
    turns = acts = errs = None

    def send_products(chunk):
        pieces = preact_half(plan, False, tabs[chunk], *rows[chunk], enc_weight, 1)
        sends[chunk] = [swap(piece, "tok", 1) for piece in pieces]

    def keep_products(chunk):
        keeps[chunk] = preact_half(plan, True, tabs[chunk], *rows[chunk], enc_weight, 1)[0]

    def add_norms(squares, bits):
        for bit in bits:
            squares = norm_add(plan, tabs[0], squares, swap(squares, "tok", bit))
        return squares

    def reduce_pairs(chunk):
        parts[chunk] = spread_parts(plan, pair_sum(plan, tabs[chunk], keeps[chunk], sends[chunk]))

    def activate(chunk):
        shard, positives[chunk] = shard_acts(plan, tabs[chunk], bias, parts[chunk])
        shards[chunk] = spread_shard(plan, shard)

    def gather(chunk, count=1):
        near = join(plan, tabs[chunk], shards[chunk], count)
        shards[chunk] = (near, [swap(piece, "tok", 1) for piece in near])

    def rebuild(chunk, acts):
        count = 4 if chunk else 1
        acts, own, *others = recon(plan, chunk, tabs[chunk], *shards[chunk], dec_weight, acts, count)
        sums[chunk] = (own, others)
        return acts

    def total(chunk):
        own, others = sums[chunk]
        others = [swap(plan.pin(other), "feat", 1) for other in others]
        sums[chunk] = chip_sum(plan, tabs[chunk], own, others)
        for step in rest:
            received[chunk ^ step, step] = from_chip(sums[chunk], step)

    def compare(chunk):
        others = [received[chunk, step] for step in rest]
        near, *pieces = errors(plan, tabs[chunk], sums[chunk], back, rows[chunk], others, 4 if chunk else 1)
        fresh[chunk] = (near, pieces)

    def back_send(chunk):
        near, parts = fresh[chunk]
        fresh[chunk] = (near, [swap(plan.pin(part), "feat", 1) for part in parts])
        after = fresh[chunk][1] if chunk else ()
        sends[chunk] = [swap(act_send(plan, tabs[chunk], near, dec_weight, after), "tok", 1)]

    def back_keep(chunk, errs):
        errs, keeps[chunk] = act_keep(plan, chunk, tabs[chunk], *fresh[chunk], dec_weight, errs)
        return errs

    def differentiate(chunk):
        shard = shard_grads(plan, tabs[chunk], norm_sum, positives[chunk], parts[chunk])
        shards[chunk] = spread_shard(plan, shard)

    bits = [1 << i for i in range((plan.toks - 1).bit_length())]
    send_products(0)
    keep_products(0)
    squares = square_sums(plan, tabs[0], dec_weight)
    reduce_pairs(0)
    for chunk in rest:
        tabs[chunk] = slot_table(plan, both(plan.pin(lists[chunk])))
    activate(0)
    for chunk in rest:
        rows[chunk] = [near_memory(value) for value in both(plan.pin(arriving[chunk]))]
        send_products(chunk)
        keep_products(chunk)
    gather(0)
    for chunk in chips:
        turns = turned(plan, chunk, tabs[chunk], *rows[chunk], turns)
    for chunk in rest:
        reduce_pairs(chunk)
    acts = rebuild(0, acts)
    for chunk in rest:
        activate(chunk)
    total(0)
    for chunk in rest:
        gather(chunk)
    squares = add_norms(squares, bits[1:-1])
    order = order_table(plan, [tabs[chunk] for chunk in chips])
    for chunk in rest:
        acts = rebuild(chunk, acts)
    squares = add_norms(squares, bits[:1])
    for chunk in rest:
        total(chunk)

    for chunk in rest:
        compare(chunk)
        back_send(chunk)
        errs = back_keep(chunk, errs)
    norm_sum, inverse = norms(plan, tabs[0], squares, swap(squares, "tok", bits[-1]))
    for chunk in rest:
        reduce_pairs(chunk)
    compare(0)
    for chunk in rest:
        differentiate(chunk)
    back_send(0)
    errs = back_keep(0, errs)
    reduce_pairs(0)
    values = (order, inverse, dec_weight, acts, errs)
    out_dec = grad_dec(plan, 0, 4, *values)
    for chunk in rest:
        gather(chunk)
    differentiate(0)
    out_dec = grad_dec(plan, 4, 4, *values, into=out_dec)
    gather(0)
    out_dec = grad_dec(plan, 8, LB - 8, *values, into=out_dec)
    out_enc = grad_enc(plan, order, [side[0] for chunk in chips for side in shards[chunk]], near_memory(turns))
    return (out_enc, out_dec)


def solution(mesh):
    return jax.shard_map(
        on_device,
        mesh=mesh,
        in_specs=(
            P("feat", "tok"),
            P("tok", "feat"),
            P("feat"),
            P("feat", "tok"),
            P("tok"),
            P("feat", None),
            P("feat"),
        ),
        out_specs=(P("tok", "feat"), P("feat", "tok")),
        check_vma=False,
    )
```

```python
import functools

import jax
import jax.numpy as jnp
from jax import lax
from jax.experimental import pallas as pl
from jax.experimental.pallas import tpu as pltpu
from jax.sharding import PartitionSpec as P

D = 8192
FB = 256
TB = 128
K = 8
LB = 11


norm_eps = 1e-06
sparsity_weight = 0.2
GRAIN = 16
VMEM = 24 * 2**20
DEPTH = 6

f32 = jnp.float32
bf16 = jnp.bfloat16


def swap(value, axis, mask):
    size = lax.axis_size(axis)
    return lax.ppermute(value, axis, [(i, i ^ mask) for i in range(size)])


def full(shape):
    return pl.BlockSpec(shape, lambda *_: (0,) * len(shape), pipeline_mode=pl.Buffered(1))


def like(shape, dtype=bf16):
    return jax.ShapeDtypeStruct(tuple(shape), dtype)


def far_memory(value):
    return pltpu.with_memory_space_constraint(value, pltpu.HBM)


def near_memory(value):
    return pltpu.with_memory_space_constraint(value, pltpu.VMEM)


class Plan:
    def __init__(self, groups, toks, rows, columns):
        self.groups, self.toks, self.rows, self.columns = groups, toks, rows, columns
        self.chips = groups // 2
        self.line = toks // 2
        self.blocks = rows // TB
        self.cap = (3 * self.blocks * K + 2 * groups - 1) // (2 * groups)
        unit = max(2, toks * GRAIN // TB)
        self.slots = -(-2 * self.cap // unit) * unit
        self.half = self.slots // 2
        self.shard = self.slots * TB // toks
        self.block = self.slots
        self.live = 2 * self.slots
        self.pair = 3 * self.slots
        self.place = self.pair + 1
        self.size = self.pair + 2
        self.every = self.chips * self.slots
        self.start = 2 * self.every
        self.cursor = self.start + LB + 1
        self.pair_all = self.cursor + LB
        self.place_all = self.pair_all + 1
        self.size_all = self.pair_all + 2
        self.trail = []

    def pin(self, value):
        return lax.optimization_barrier((value, self.trail))[0]

    def launch(
        self, kernel, name, grid, tab, ins, outs, scratch=(), into=None, after=()
    ):
        arrays, specs = [pltpu.with_memory_space_constraint(tab, pltpu.SMEM)], []
        for value, spec in ins:
            arrays.append(value)
            specs.append(full(value.shape) if spec is None else spec)
        extra = [*([] if into is None else [into]), *self.trail, *after]
        count = len(specs)

        def body(tab, *refs):
            kernel(tab, *refs[:count], *refs[count + len(extra) :])

        made = pl.pallas_call(
            body,
            grid_spec=pltpu.PrefetchScalarGridSpec(
                num_scalar_prefetch=1,
                grid=grid,
                in_specs=specs + [pl.BlockSpec(memory_space=pl.ANY)] * len(extra),
                out_specs=[full(shape.shape) if spec is None else spec for shape, spec in outs],
                scratch_shapes=list(scratch),
            ),
            out_shape=[shape for shape, _ in outs],
            input_output_aliases={} if into is None else {count + 1: 0},
            compiler_params=pltpu.CompilerParams(vmem_limit_bytes=VMEM),
            cost_estimate=pl.CostEstimate(flops=1, bytes_accessed=1, transcendentals=0),
            name=name,
        )(*arrays, *extra)
        self.trail = [made[-1]]
        return made


def table_kernel(plan, ids_near, ids_far, *refs):
    tab = refs[-1]
    feat, tok = lax.axis_index("feat"), lax.axis_index("tok")
    tab[plan.pair] = tok % 2
    tab[plan.place] = tok // 2
    last = jnp.int32(0)
    for core, ids in enumerate((ids_near, ids_far)):
        base = core * plan.half

        def entry(i, carry):
            used, last = carry
            name = ids[i // K, i % K]
            hit = (name >= feat * LB) & (name < feat * LB + LB)
            local = jnp.where(hit, name - feat * LB, last)

            @pl.when(hit)
            def _():
                tab[base + used] = core * plan.blocks + i // K
                tab[plan.block + base + used] = local
                tab[plan.live + base + used] = 1

            return used + hit.astype(jnp.int32), local

        used, last = lax.fori_loop(0, plan.blocks * K, entry, (jnp.int32(0), last))

        def empty(i, last):
            tab[base + i] = core * plan.blocks
            tab[plan.block + base + i] = last
            tab[plan.live + base + i] = 0
            return last

        lax.fori_loop(used, plan.half, empty, last)


def slot_table(plan, ids):
    smem = pl.BlockSpec(memory_space=pltpu.SMEM)
    tab = pl.pallas_call(
        functools.partial(table_kernel, plan),
        out_shape=pltpu.SMEM((plan.size,), jnp.int32),
        in_specs=[smem] * 2 + [pl.BlockSpec(memory_space=pl.ANY)] * len(plan.trail),
        out_specs=smem,
        name="slot_table",
    )(*ids, *plan.trail)
    plan.trail = [tab]
    return tab


def order_kernel(plan, *refs):
    tabs, every = refs[:-1], refs[-1]
    every[plan.pair_all] = tabs[0][plan.pair]
    every[plan.place_all] = tabs[0][plan.place]
    for i in range(LB + 1):
        every[plan.start + i] = 0
    for tab in tabs:

        def count(i, carry):
            at = plan.start + tab[plan.block + i] + 1
            every[at] = every[at] + tab[plan.live + i]
            return carry

        lax.fori_loop(0, plan.slots, count, 0)
    for i in range(LB):
        every[plan.start + i + 1] = every[plan.start + i] + every[plan.start + i + 1]
        every[plan.cursor + i] = every[plan.start + i]
    for chunk, tab in enumerate(tabs):

        def put(i, carry):
            @pl.when(tab[plan.live + i] > 0)
            def _():
                block = tab[plan.block + i]
                at = every[plan.cursor + block]
                every[at] = chunk * plan.slots + i
                every[plan.every + at] = chunk * 2 * plan.blocks + tab[i]
                every[plan.cursor + block] = at + 1

            return carry

        lax.fori_loop(0, plan.slots, put, 0)


def order_table(plan, tabs):
    smem = pl.BlockSpec(memory_space=pltpu.SMEM)
    every = pl.pallas_call(
        functools.partial(order_kernel, plan),
        out_shape=pltpu.SMEM((plan.size_all,), jnp.int32),
        in_specs=[smem] * len(tabs),
        out_specs=smem,
        name="order_table",
    )(*[plan.pin(tab) for tab in tabs])
    plan.trail = [every]
    return every


def block_copy(tab, at, weight, decoder, held, sems, i):
    rows = pl.ds(pl.multiple_of(tab[at] * FB, FB), FB)
    source = weight.at[rows, :] if decoder else weight.at[:, rows]
    return pltpu.make_async_copy(source, held.at[i], sems.at[i])


def half_loop(plan, own, decoder, tab, rows, base_row, weight, outs, held, sems):
    base = (tab[plan.pair] if own else 1 - tab[plan.pair]) * plan.half

    def copy(i):
        return block_copy(tab, plan.block + base + i, weight, decoder, held, sems, i)

    def start(i, carry):
        @pl.when(tab[plan.live + base + i] > 0)
        def _():
            copy(i).start()

        return carry

    def multiply(out, first, i, carry):
        live = tab[plan.live + base + i] > 0
        token = tab[base + i]
        to = pl.ds(pl.multiple_of((i - first) * TB, TB), TB)

        @pl.when(live)
        def _():
            copy(i).wait()
            at = pl.ds(pl.multiple_of((token - base_row) * TB, TB), TB)
            out[to, :] = lax.dot_general(
                rows[at, :],
                held[i],
                (((1,), (1 if decoder else 0,)), ((), ())),
                preferred_element_type=f32,
            ).astype(out.dtype)

        @pl.when(jnp.logical_not(live))
        def _():
            out[to, :] = jnp.zeros((TB, FB), out.dtype)

        return carry

    def start_all():
        lax.fori_loop(0, plan.half, start, 0)

    def multiply_all():
        size = plan.half // len(outs)
        for piece, out in enumerate(outs):
            step = functools.partial(multiply, out, piece * size)
            lax.fori_loop(piece * size, (piece + 1) * size, step, 0)

    return start_all, multiply_all


def hbm():
    return pl.BlockSpec(memory_space=pltpu.HBM)


def half_scratch(plan, decoder):
    shape = (FB, plan.columns) if decoder else (plan.columns, FB)
    return [pltpu.VMEM((plan.half, *shape), bf16), pltpu.SemaphoreType.DMA((plan.half,))]


def preact_kernel(plan, own, tab, near, far, weight, *refs):
    outs, (rows, held, row_sem, sems) = refs[:-4], refs[-4:]
    home = tab[plan.pair] if own else 1 - tab[plan.pair]
    moves = [pltpu.make_async_copy(ref, rows, row_sem) for ref in (near, far)]
    for core, move in enumerate(moves):
        pl.when(home == core)(move.start)
    base_row = home * plan.blocks
    start, multiply = half_loop(plan, own, False, tab, rows, base_row, weight, outs, held, sems)
    start()
    moves[0].wait()
    multiply()


def halves(plan, dtype, count):
    return [(like((plan.half * TB // count, FB), dtype), None)] * count


def preact_half(plan, own, tab, near, far, weight, count):
    held, sems = half_scratch(plan, False)
    return plan.launch(
        functools.partial(preact_kernel, plan, own),
        "preact_half",
        (1,),
        tab,
        [(near, hbm()), (far, hbm()), (weight, hbm())],
        halves(plan, f32 if own else bf16, count),
        [
            pltpu.VMEM((plan.rows, plan.columns), bf16),
            held,
            pltpu.SemaphoreType.DMA,
            sems,
        ],
    )


def act_send_kernel(plan, tab, weight, near, *refs):
    base_row = (1 - tab[plan.pair]) * plan.blocks
    outs, (held, sems) = refs[:-2], refs[-2:]
    start, multiply = half_loop(plan, False, True, tab, near, base_row, weight, outs, held, sems)
    start()
    multiply()


def chunk_rows(plan, chunk):
    return pl.BlockSpec(
        (2 * plan.rows, plan.columns), lambda *_: (chunk, 0), pipeline_mode=pl.Buffered(1)
    )


def act_send(plan, tab, near, weight, after):
    return plan.launch(
        functools.partial(act_send_kernel, plan),
        "act_grad_send",
        (1,),
        tab,
        [(weight, hbm()), (near, None)],
        halves(plan, bf16, 1),
        half_scratch(plan, True),
        after=after,
    )[0]


def act_keep_kernel(plan, count, tab, weight, near, *refs):
    parts, errs, outs = refs[:count], refs[count], refs[count + 1 : -2]
    start, multiply = half_loop(plan, True, True, tab, errs, 0, weight, outs, *refs[-2:])
    start()
    here = pl.multiple_of((1 - tab[plan.pair]) * plan.rows, TB)
    errs[pl.ds(here, plan.rows), :] = near[...]
    size = plan.rows // count
    for i, part in enumerate(parts):
        there = pl.multiple_of(tab[plan.pair] * plan.rows + i * size, GRAIN)
        errs[pl.ds(there, size), :] = part[...]
    multiply()


def act_keep(plan, chunk, tab, near, parts, weight, errs):
    return plan.launch(
        functools.partial(act_keep_kernel, plan, len(parts)),
        "act_grad_keep",
        (1,),
        tab,
        [(weight, hbm()), (near, None)] + [(part, None) for part in parts],
        [
            (like((plan.chips * 2 * plan.rows, plan.columns)), chunk_rows(plan, chunk)),
            *halves(plan, f32, 1),
        ],
        half_scratch(plan, True),
        into=errs,
    )


def pair_sum_kernel(plan, count, tab, keep, *refs):
    recvs, outs = refs[:count], refs[count:]
    size = plan.line // count
    for i, out in enumerate(outs):
        place = tab[plan.place] ^ i
        rows = pl.ds(pl.multiple_of(place * plan.shard, GRAIN), plan.shard)
        for piece, recv in enumerate(recvs):

            @pl.when(place // size == piece)
            def _():
                at = pl.multiple_of((place % size) * plan.shard, GRAIN)
                there = recv[pl.ds(at, plan.shard), :].astype(f32)
                out[...] = (keep[rows, :] + there).astype(out.dtype)


def pair_sum(plan, tab, keep, recvs):
    shape = (plan.shard, FB)
    return plan.launch(
        functools.partial(pair_sum_kernel, plan, len(recvs)),
        "pair_sum",
        (1,),
        tab,
        [(keep, None)] + [(recv, None) for recv in recvs],
        [(like(shape, bf16 if i else f32), None) for i in range(plan.line)],
    )


def grain_slot(plan, tab, grain):
    shard = tab[plan.pair] * plan.line + tab[plan.place]
    slot = (shard * plan.shard + grain * GRAIN) // TB
    return tab[plan.block + slot], tab[plan.live + slot] > 0


def act_kernel(plan, tab, bias, *refs):
    parts, (acts, positives) = refs[:-2], refs[-2:]
    for grain in range(plan.shard // GRAIN):
        block, live = grain_slot(plan, tab, grain)
        rows = slice(grain * GRAIN, (grain + 1) * GRAIN)
        total = bias[pl.ds(block, 1), :]
        for part in parts:
            total = total + part[rows, :].astype(f32)
        positive = jnp.where(live, jnp.maximum(total, 0.0), 0.0)
        positives[rows, :] = positive
        acts[rows, :] = (positive * positive).astype(bf16)


def shard_acts(plan, tab, bias, parts):
    shape = (plan.shard, FB)
    return plan.launch(
        functools.partial(act_kernel, plan),
        "shard_acts",
        (1,),
        tab,
        [(bias, None)] + [(part, None) for part in parts],
        [(like(shape), None), (pltpu.VMEM(shape, f32), None)],
    )


def grad_kernel(plan, tab, norms, positives, *refs):
    parts, out = refs[:-1], refs[-1]
    for grain in range(plan.shard // GRAIN):
        block, live = grain_slot(plan, tab, grain)
        rows = slice(grain * GRAIN, (grain + 1) * GRAIN)
        total = sparsity_weight * norms[pl.ds(block, 1), :]
        for part in parts:
            total = total + part[rows, :].astype(f32)
        out[rows, :] = jnp.where(live, total * 2.0 * positives[rows, :], 0.0).astype(bf16)


def shard_grads(plan, tab, norms, positives, parts):
    return plan.launch(
        functools.partial(grad_kernel, plan),
        "shard_grads",
        (1,),
        tab,
        [(norms, None), (near_memory(positives), None)] + [(part, None) for part in parts],
        [(like((plan.shard, FB)), None)],
    )[0]


def assemble(plan, pair, place, near, far, out, base):
    for side, refs in enumerate((near, far)):
        size = plan.line // len(refs)
        for i in range(plan.line):
            shard = (pair ^ side) * plan.line + (place ^ i)
            at = pl.multiple_of(base + shard * plan.shard, GRAIN)
            part = slice(i % size * plan.shard, (i % size + 1) * plan.shard)
            out[pl.ds(at, plan.shard), :] = refs[i // size][part, :]


def recon_kernel(plan, count, tab, *refs):
    near, far = refs[:count], refs[count : 2 * count]
    weight, acts, total, *refs = refs[2 * count :]
    others, (held, sems) = refs[:-2], refs[-2:]
    depth = held.shape[0]

    def copy(i):
        return block_copy(tab, plan.block + i, weight, True, held, sems, i % depth)

    def start(i, carry):
        @pl.when(tab[plan.live + i] > 0)
        def _():
            copy(i).start()

        return carry

    def multiply(i, carry):
        @pl.when(tab[plan.live + i] > 0)
        def _():
            at = pl.ds(pl.multiple_of(tab[i] * TB, TB), TB)
            rows = pl.ds(pl.multiple_of(i * TB, TB), TB)
            copy(i).wait()
            total[at, :] += jnp.dot(acts[rows, :], held[i % depth], preferred_element_type=f32)

        @pl.when(i + depth < plan.slots)
        def _():
            start(i + depth, 0)

        return carry

    lax.fori_loop(0, depth, start, 0)
    assemble(plan, tab[plan.pair], tab[plan.place], near, far, acts, 0)
    total[...] = jnp.zeros_like(total)
    lax.fori_loop(0, plan.slots, multiply, 0)
    size = plan.rows // len(others)
    for i, other in enumerate(others):
        at = pl.multiple_of(tab[plan.pair] * plan.rows + i * size, GRAIN)
        other[...] = total[pl.ds(at, size), :].astype(bf16)


def recon(plan, chunk, tab, near, far, dec_weight, acts, pieces):
    depth = min(DEPTH, plan.slots)
    acts_shape = (plan.slots * TB, FB)
    piece = like((plan.rows // pieces, plan.columns))
    return plan.launch(
        functools.partial(recon_kernel, plan, len(near)),
        "recon",
        (1,),
        tab,
        [(value, None) for value in (*near, *far)] + [(dec_weight, hbm())],
        [
            (
                like((plan.every * TB, FB)),
                pl.BlockSpec(acts_shape, lambda *_: (chunk, 0), pipeline_mode=pl.Buffered(1)),
            ),
            (like((2 * plan.rows, plan.columns), f32), None),
        ]
        + [(piece, None)] * pieces,
        [
            pltpu.VMEM((depth, FB, plan.columns), bf16),
            pltpu.SemaphoreType.DMA((depth,)),
        ],
        into=acts,
    )


def column(row):
    return jnp.broadcast_to(row, (TB, row.shape[1])).T[:, :1]


def square_kernel(tab, weight, out, held, sems):
    depth = held.shape[0]

    def copy(i):
        rows = pl.ds(pl.multiple_of(i * FB, FB), FB)
        return pltpu.make_async_copy(weight.at[rows, :], held.at[i % depth], sems.at[i % depth])

    for i in range(depth):
        copy(i).start()

    def add(i, carry):
        copy(i).wait()
        value = held[i % depth].astype(f32)
        total = jnp.sum(value * value, axis=1, keepdims=True)
        out[pl.ds(i, 1), :] = jnp.broadcast_to(total, (FB, TB)).T[:1, :]

        @pl.when(i + depth < LB)
        def _():
            copy(i + depth).start()

        return carry

    lax.fori_loop(0, LB, add, 0)


def square_sums(plan, tab, dec_weight):
    return plan.launch(
        square_kernel,
        "square_sums",
        (1,),
        tab,
        [(dec_weight, hbm())],
        [(like((LB, FB), f32), None)],
        [pltpu.VMEM((DEPTH, FB, plan.columns), bf16), pltpu.SemaphoreType.DMA((DEPTH,))],
    )[0]


def turn_kernel(tab, near, far, out, mark):
    mark[...] = jnp.zeros_like(mark)
    rows = near.shape[0]
    out[:, :rows] = near[...].T
    out[:, rows:] = far[...].T


def turned(plan, chunk, tab, near, far, into):
    width = min(1024, plan.columns)
    block = pl.BlockSpec((plan.rows, width), lambda i, tab: (0, i))
    return plan.launch(
        turn_kernel,
        "turn_rows",
        (plan.columns // width,),
        tab,
        [(near, block), (far, block)],
        [
            (
                pltpu.HBM((plan.columns, plan.chips * 2 * plan.rows), bf16),
                pl.BlockSpec((width, 2 * plan.rows), lambda i, tab: (i, chunk)),
            ),
            (like((8, TB), f32), None),
        ],
        into=into,
    )[0]


def norm_add_kernel(tab, here, there, out):
    out[...] = here[...] + there[...]


def norm_add(plan, tab, here, there):
    return plan.launch(
        norm_add_kernel,
        "norm_add",
        (1,),
        tab,
        [(here, None), (there, None)],
        [(like(here.shape, f32), None)],
    )[0]


def norm_kernel(tab, here, there, total, inverse):
    norm = jnp.sqrt(here[...] + norm_eps)
    total[...] = norm + jnp.sqrt(there[...] + norm_eps)
    inverse[...] = 1.0 / norm


def norms(plan, tab, here, there):
    return plan.launch(
        norm_kernel,
        "norms",
        (1,),
        tab,
        [(here, None), (there, None)],
        [(like(here.shape, f32), None)] * 2,
    )


def two_slots(tab, plan, i, last):
    more = i + 1 < last
    j = jnp.where(more, i + 1, i)

    def at(value):
        return pl.ds(pl.multiple_of(value * TB, TB), TB)

    return more, at(tab[i]), at(tab[j]), at(tab[plan.every + i]), at(tab[plan.every + j])


def grad_dec_kernel(plan, base, tab, inverse, weight, acts, errs, out, mark, total, sums):
    mark[...] = jnp.zeros_like(mark)
    block = base + pl.program_id(0)
    first, last = tab[plan.start + block], tab[plan.start + block + 1]

    def load(i):
        more, here, there, token, other = two_slots(tab, plan, i, last)
        second = jnp.where(more, acts[there, :], jnp.zeros((TB, FB), bf16))
        these = jnp.concatenate([acts[here, :], second], axis=0).T
        rows = jnp.concatenate([errs[token, :], errs[other, :]], axis=0)
        count = jnp.dot(these, jnp.ones((2 * TB, TB), bf16), preferred_element_type=f32)
        return count, jnp.dot(these, rows, preferred_element_type=f32)

    def finish(count, value):
        scale = sparsity_weight * count[:, :1] * column(inverse[pl.ds(block, 1), :])
        out[...] = (value + scale * weight[...].astype(f32)).astype(bf16)

    @pl.when((last > first) & (last - first <= 2))
    def _():
        finish(*load(first))

    @pl.when((last - first > 2) & (last - first <= 4))
    def _():
        count, value = load(first)
        more, rest = load(first + 2)
        finish(count + more, value + rest)

    @pl.when(last - first > 4)
    def _():
        count, value = load(first)
        sums[...] = count
        total[...] = value

        def add(i, carry):
            count, value = load(first + 2 * i)
            sums[...] += count
            total[...] += value
            return carry

        lax.fori_loop(1, (last - first + 1) // 2, add, 0)
        finish(sums[...], total[...])

    @pl.when(first >= last)
    def _():
        out[...] = jnp.zeros(out.shape, bf16)


def grad_dec(plan, base, count, tab, inverse, dec_weight, acts, errs, into=None):
    shape = (FB, plan.columns)
    spec = pl.BlockSpec(shape, lambda i, tab: (base + i, 0))
    return plan.launch(
        functools.partial(grad_dec_kernel, plan, base),
        "grad_dec",
        (count,),
        tab,
        [(inverse, None), (dec_weight, spec), (acts, None), (errs, None)],
        [(like((LB * FB, plan.columns)), spec), (like((8, TB), f32), None)],
        [pltpu.VMEM(shape, f32), pltpu.VMEM((FB, TB), f32)],
        into=into,
    )[0]


def grad_enc_kernel(plan, tab, rows, *refs):
    grads, (out, total, every) = refs[: 2 * plan.chips], refs[2 * plan.chips :]
    block = pl.program_id(0)

    @pl.when(block == 0)
    def _():
        for chunk in range(plan.chips):
            near, far = grads[2 * chunk], grads[2 * chunk + 1]
            base = chunk * plan.slots * TB
            assemble(plan, tab[plan.pair_all], tab[plan.place_all], [near], [far], every, base)

    first, last = tab[plan.start + block], tab[plan.start + block + 1]

    def load(i):
        more, here, there, token, other = two_slots(tab, plan, i, last)
        second = jnp.where(more, every[there, :], jnp.zeros((TB, FB), bf16))
        right = jnp.concatenate([every[here, :], second], axis=0)
        left = jnp.concatenate([rows[:, token], rows[:, other]], axis=1)
        return jnp.dot(left, right, preferred_element_type=f32)

    @pl.when(last - first > 4)
    def _():
        total[...] = load(first)

        def add(i, carry):
            total[...] += load(first + 2 * i)
            return carry

        lax.fori_loop(1, (last - first + 1) // 2, add, 0)
        out[...] = total[...].astype(bf16)

    @pl.when((last > first) & (last - first <= 2))
    def _():
        out[...] = load(first).astype(bf16)

    @pl.when((last - first > 2) & (last - first <= 4))
    def _():
        out[...] = (load(first) + load(first + 2)).astype(bf16)

    @pl.when(last == first)
    def _():
        out[...] = jnp.zeros(out.shape, bf16)


def grad_enc(plan, tab, grads, rows):
    shape = (plan.columns, FB)
    return plan.launch(
        functools.partial(grad_enc_kernel, plan),
        "grad_enc",
        (LB,),
        tab,
        [(value, None) for value in (rows, *grads)],
        [(like((plan.columns, LB * FB)), pl.BlockSpec(shape, lambda i, tab: (0, i)))],
        [pltpu.VMEM(shape, f32), pltpu.VMEM((plan.every * TB, FB), bf16)],
    )[0]


def join_kernel(plan, tab, *refs):
    parts, outs = refs[: plan.line], refs[plan.line :]
    size = plan.line // len(outs)
    for i, part in enumerate(parts):
        rows = slice(i % size * plan.shard, (i % size + 1) * plan.shard)
        outs[i // size][rows, :] = part[...]


def join(plan, tab, parts, count):
    return plan.launch(
        functools.partial(join_kernel, plan),
        "join_shards",
        (1,),
        tab,
        [(part, None) for part in parts],
        halves(plan, bf16, count),
    )


def chip_sum_kernel(plan, tab, both, *refs):
    others, total = refs[:-1], refs[-1]
    size = plan.rows // len(others)
    for i, other in enumerate(others):
        at = pl.multiple_of((1 - tab[plan.pair]) * plan.rows + i * size, GRAIN)
        value = both[pl.ds(at, size), :] + other[...].astype(f32)
        total[i * size : (i + 1) * size, :] = value.astype(bf16)


def chip_sum(plan, tab, both, others):
    return plan.launch(
        functools.partial(chip_sum_kernel, plan),
        "chip_sum",
        (1,),
        tab,
        [(both, None)] + [(other, None) for other in others],
        [(like((plan.rows, plan.columns)), None)],
    )[0]


def error_kernel(plan, pieces, tab, total, bias, near_rows, far_rows, *refs):
    others, near, parts = refs[: -1 - pieces], refs[-1 - pieces], refs[-pieces:]
    size = plan.rows // pieces
    for core, rows in enumerate((near_rows, far_rows)):

        @pl.when(1 - tab[plan.pair] == core)
        def _():
            for i, part in enumerate(parts):
                at = slice(i * size, (i + 1) * size)
                value = total[at, :].astype(f32)
                for other in others:
                    value = value + other[at, :].astype(f32)
                error = value + bias[...] - rows[at, :].astype(f32)
                error = (error * TB ** (-0.5)).astype(bf16)
                near[at, :] = error
                part[...] = error


def errors(plan, tab, total, bias, rows, received, pieces):
    piece = like((plan.rows // pieces, plan.columns))
    return plan.launch(
        functools.partial(error_kernel, plan, pieces),
        "errors",
        (1,),
        tab,
        [(value, None) for value in (total, bias, *rows, *received)],
        [(like(total.shape), None)] + [(piece, None)] * pieces,
    )


def spread_parts(plan, parts):
    return [parts[0]] + [swap(parts[i], "tok", 2 * i) for i in range(1, plan.line)]


def spread_shard(plan, shard):
    return [shard] + [swap(shard, "tok", 2 * i) for i in range(1, plan.line)]


def on_device(resid, enc_weight, enc_bias, dec_weight, dec_bias, active_ids, active_count):
    plan = Plan(lax.axis_size("feat"), lax.axis_size("tok"), *resid.shape)
    chips = range(plan.chips)
    rest = list(chips[1:])
    enc_weight, dec_weight = far_memory(enc_weight), far_memory(dec_weight)
    bias = enc_bias.reshape(LB, FB)
    back = dec_bias[None, :]

    def from_chip(value, chunk):
        return swap(value, "feat", 2 * chunk)

    def both(value):
        return value, swap(value, "feat", 1)

    entries = jnp.where(jnp.arange(K)[None, :] < active_count[:, None], active_ids, -1)
    entries, moving = lax.optimization_barrier((entries, resid))
    lists = {chunk: from_chip(entries, chunk) for chunk in rest}
    tabs = {0: slot_table(plan, both(entries))}
    rows = {0: [far_memory(resid), near_memory(swap(resid, "feat", 1))]}
    arriving = {chunk: from_chip(moving, chunk) for chunk in rest}
    sends, keeps, parts, shards, positives, sums, received, fresh = ({} for _ in range(8))
    turns = acts = errs = None

    def send_products(chunk):
        pieces = preact_half(plan, False, tabs[chunk], *rows[chunk], enc_weight, 1)
        sends[chunk] = [swap(piece, "tok", 1) for piece in pieces]

    def keep_products(chunk):
        keeps[chunk] = preact_half(plan, True, tabs[chunk], *rows[chunk], enc_weight, 1)[0]

    def add_norms(squares, bits):
        for bit in bits:
            squares = norm_add(plan, tabs[0], squares, swap(squares, "tok", bit))
        return squares

    def reduce_pairs(chunk):
        parts[chunk] = spread_parts(plan, pair_sum(plan, tabs[chunk], keeps[chunk], sends[chunk]))

    def activate(chunk):
        shard, positives[chunk] = shard_acts(plan, tabs[chunk], bias, parts[chunk])
        shards[chunk] = spread_shard(plan, shard)

    def gather(chunk, count=1):
        near = join(plan, tabs[chunk], shards[chunk], count)
        shards[chunk] = (near, [swap(piece, "tok", 1) for piece in near])

    def rebuild(chunk, acts):
        count = 4 if chunk else 1
        acts, own, *others = recon(plan, chunk, tabs[chunk], *shards[chunk], dec_weight, acts, count)
        sums[chunk] = (own, others)
        return acts

    def total(chunk):
        own, others = sums[chunk]
        others = [swap(plan.pin(other), "feat", 1) for other in others]
        sums[chunk] = chip_sum(plan, tabs[chunk], own, others)
        for step in rest:
            received[chunk ^ step, step] = from_chip(sums[chunk], step)

    def compare(chunk):
        others = [received[chunk, step] for step in rest]
        near, *pieces = errors(plan, tabs[chunk], sums[chunk], back, rows[chunk], others, 4 if chunk else 1)
        fresh[chunk] = (near, pieces)

    def back_send(chunk):
        near, parts = fresh[chunk]
        fresh[chunk] = (near, [swap(plan.pin(part), "feat", 1) for part in parts])
        after = fresh[chunk][1] if chunk else ()
        sends[chunk] = [swap(act_send(plan, tabs[chunk], near, dec_weight, after), "tok", 1)]

    def back_keep(chunk, errs):
        errs, keeps[chunk] = act_keep(plan, chunk, tabs[chunk], *fresh[chunk], dec_weight, errs)
        return errs

    def differentiate(chunk):
        shard = shard_grads(plan, tabs[chunk], norm_sum, positives[chunk], parts[chunk])
        shards[chunk] = spread_shard(plan, shard)

    bits = [1 << i for i in range((plan.toks - 1).bit_length())]
    send_products(0)
    keep_products(0)
    squares = square_sums(plan, tabs[0], dec_weight)
    reduce_pairs(0)
    for chunk in rest:
        tabs[chunk] = slot_table(plan, both(plan.pin(lists[chunk])))
    activate(0)
    for chunk in rest:
        rows[chunk] = [near_memory(value) for value in both(plan.pin(arriving[chunk]))]
        send_products(chunk)
        keep_products(chunk)
    gather(0)
    for chunk in chips:
        turns = turned(plan, chunk, tabs[chunk], *rows[chunk], turns)
    for chunk in rest:
        reduce_pairs(chunk)
    acts = rebuild(0, acts)
    for chunk in rest:
        activate(chunk)
    total(0)
    for chunk in rest:
        gather(chunk)
    squares = add_norms(squares, bits[1:-1])
    order = order_table(plan, [tabs[chunk] for chunk in chips])
    for chunk in rest:
        acts = rebuild(chunk, acts)
    squares = add_norms(squares, bits[:1])
    for chunk in rest:
        total(chunk)

    for chunk in rest:
        compare(chunk)
        back_send(chunk)
        errs = back_keep(chunk, errs)
    norm_sum, inverse = norms(plan, tabs[0], squares, swap(squares, "tok", bits[-1]))
    for chunk in rest:
        reduce_pairs(chunk)
    compare(0)
    for chunk in rest:
        differentiate(chunk)
    back_send(0)
    errs = back_keep(0, errs)
    reduce_pairs(0)
    values = (order, inverse, dec_weight, acts, errs)
    out_dec = grad_dec(plan, 0, 4, *values)
    for chunk in rest:
        gather(chunk)
    differentiate(0)
    out_dec = grad_dec(plan, 4, 4, *values, into=out_dec)
    gather(0)
    out_dec = grad_dec(plan, 8, LB - 8, *values, into=out_dec)
    out_enc = grad_enc(plan, order, [side[0] for chunk in chips for side in shards[chunk]], near_memory(turns))
    return (out_enc, out_dec)


def solution(mesh):
    return jax.shard_map(
        on_device,
        mesh=mesh,
        in_specs=(
            P("feat", "tok"),
            P("tok", "feat"),
            P("feat"),
            P("feat", "tok"),
            P("tok"),
            P("feat", None),
            P("feat"),
        ),
        out_specs=(P("tok", "feat"), P("feat", "tok")),
        check_vma=False,
    )
```

```python
import functools

import jax
import jax.numpy as jnp
from jax import lax
from jax.experimental import pallas as pl
from jax.experimental.pallas import tpu as pltpu
from jax.sharding import PartitionSpec as P

D = 8192
FB = 256
TB = 128
K = 8
LB = 11


norm_eps = 1e-06
sparsity_weight = 0.2
GRAIN = 16
VMEM = 24 * 2**20
DEPTH = 6

f32 = jnp.float32
bf16 = jnp.bfloat16


def swap(value, axis, mask):
    size = lax.axis_size(axis)
    return lax.ppermute(value, axis, [(i, i ^ mask) for i in range(size)])


def full(shape):
    return pl.BlockSpec(shape, lambda *_: (0,) * len(shape), pipeline_mode=pl.Buffered(1))


def like(shape, dtype=bf16):
    return jax.ShapeDtypeStruct(tuple(shape), dtype)


def far_memory(value):
    return pltpu.with_memory_space_constraint(value, pltpu.HBM)


def near_memory(value):
    return pltpu.with_memory_space_constraint(value, pltpu.VMEM)


class Plan:
    def __init__(self, groups, toks, rows, columns):
        self.groups, self.toks, self.rows, self.columns = groups, toks, rows, columns
        self.chips = groups // 2
        self.line = toks // 2
        self.blocks = rows // TB
        self.cap = (3 * self.blocks * K + 2 * groups - 1) // (2 * groups)
        unit = max(2, toks * GRAIN // TB)
        self.slots = -(-2 * self.cap // unit) * unit
        self.half = self.slots // 2
        self.shard = self.slots * TB // toks
        self.block = self.slots
        self.live = 2 * self.slots
        self.pair = 3 * self.slots
        self.place = self.pair + 1
        self.size = self.pair + 2
        self.every = self.chips * self.slots
        self.start = 2 * self.every
        self.cursor = self.start + LB + 1
        self.pair_all = self.cursor + LB
        self.place_all = self.pair_all + 1
        self.size_all = self.pair_all + 2
        self.trail = []

    def pin(self, value):
        return lax.optimization_barrier((value, self.trail))[0]

    def launch(
        self, kernel, name, grid, tab, ins, outs, scratch=(), into=None, after=()
    ):
        arrays, specs = [pltpu.with_memory_space_constraint(tab, pltpu.SMEM)], []
        for value, spec in ins:
            arrays.append(value)
            specs.append(full(value.shape) if spec is None else spec)
        extra = [*([] if into is None else [into]), *self.trail, *after]
        count = len(specs)

        def body(tab, *refs):
            kernel(tab, *refs[:count], *refs[count + len(extra) :])

        made = pl.pallas_call(
            body,
            grid_spec=pltpu.PrefetchScalarGridSpec(
                num_scalar_prefetch=1,
                grid=grid,
                in_specs=specs + [pl.BlockSpec(memory_space=pl.ANY)] * len(extra),
                out_specs=[full(shape.shape) if spec is None else spec for shape, spec in outs],
                scratch_shapes=list(scratch),
            ),
            out_shape=[shape for shape, _ in outs],
            input_output_aliases={} if into is None else {count + 1: 0},
            compiler_params=pltpu.CompilerParams(vmem_limit_bytes=VMEM),
            cost_estimate=pl.CostEstimate(flops=1, bytes_accessed=1, transcendentals=0),
            name=name,
        )(*arrays, *extra)
        self.trail = [made[-1]]
        return made


def table_kernel(plan, ids_near, ids_far, *refs):
    tab = refs[-1]
    feat, tok = lax.axis_index("feat"), lax.axis_index("tok")
    tab[plan.pair] = tok % 2
    tab[plan.place] = tok // 2
    last = jnp.int32(0)
    for core, ids in enumerate((ids_near, ids_far)):
        base = core * plan.half

        def entry(i, carry):
            used, last = carry
            name = ids[i // K, i % K]
            hit = (name >= feat * LB) & (name < feat * LB + LB)
            local = jnp.where(hit, name - feat * LB, last)

            @pl.when(hit)
            def _():
                tab[base + used] = core * plan.blocks + i // K
                tab[plan.block + base + used] = local
                tab[plan.live + base + used] = 1

            return used + hit.astype(jnp.int32), local

        used, last = lax.fori_loop(0, plan.blocks * K, entry, (jnp.int32(0), last))

        def empty(i, last):
            tab[base + i] = core * plan.blocks
            tab[plan.block + base + i] = last
            tab[plan.live + base + i] = 0
            return last

        lax.fori_loop(used, plan.half, empty, last)


def slot_table(plan, ids):
    smem = pl.BlockSpec(memory_space=pltpu.SMEM)
    tab = pl.pallas_call(
        functools.partial(table_kernel, plan),
        out_shape=pltpu.SMEM((plan.size,), jnp.int32),
        in_specs=[smem] * 2 + [pl.BlockSpec(memory_space=pl.ANY)] * len(plan.trail),
        out_specs=smem,
        name="slot_table",
    )(*ids, *plan.trail)
    plan.trail = [tab]
    return tab


def order_kernel(plan, *refs):
    tabs, every = refs[:-1], refs[-1]
    every[plan.pair_all] = tabs[0][plan.pair]
    every[plan.place_all] = tabs[0][plan.place]
    for i in range(LB + 1):
        every[plan.start + i] = 0
    for tab in tabs:

        def count(i, carry):
            at = plan.start + tab[plan.block + i] + 1
            every[at] = every[at] + tab[plan.live + i]
            return carry

        lax.fori_loop(0, plan.slots, count, 0)
    for i in range(LB):
        every[plan.start + i + 1] = every[plan.start + i] + every[plan.start + i + 1]
        every[plan.cursor + i] = every[plan.start + i]
    for chunk, tab in enumerate(tabs):

        def put(i, carry):
            @pl.when(tab[plan.live + i] > 0)
            def _():
                block = tab[plan.block + i]
                at = every[plan.cursor + block]
                every[at] = chunk * plan.slots + i
                every[plan.every + at] = chunk * 2 * plan.blocks + tab[i]
                every[plan.cursor + block] = at + 1

            return carry

        lax.fori_loop(0, plan.slots, put, 0)


def order_table(plan, tabs):
    smem = pl.BlockSpec(memory_space=pltpu.SMEM)
    every = pl.pallas_call(
        functools.partial(order_kernel, plan),
        out_shape=pltpu.SMEM((plan.size_all,), jnp.int32),
        in_specs=[smem] * len(tabs),
        out_specs=smem,
        name="order_table",
    )(*[plan.pin(tab) for tab in tabs])
    plan.trail = [every]
    return every


def block_copy(tab, at, weight, decoder, held, sems, i):
    rows = pl.ds(pl.multiple_of(tab[at] * FB, FB), FB)
    source = weight.at[rows, :] if decoder else weight.at[:, rows]
    return pltpu.make_async_copy(source, held.at[i], sems.at[i])


def half_loop(plan, own, decoder, tab, rows, base_row, weight, outs, held, sems):
    base = (tab[plan.pair] if own else 1 - tab[plan.pair]) * plan.half

    def copy(i):
        return block_copy(tab, plan.block + base + i, weight, decoder, held, sems, i)

    def start(i, carry):
        @pl.when(tab[plan.live + base + i] > 0)
        def _():
            copy(i).start()

        return carry

    def multiply(out, first, i, carry):
        live = tab[plan.live + base + i] > 0
        token = tab[base + i]
        to = pl.ds(pl.multiple_of((i - first) * TB, TB), TB)

        @pl.when(live)
        def _():
            copy(i).wait()
            at = pl.ds(pl.multiple_of((token - base_row) * TB, TB), TB)
            out[to, :] = lax.dot_general(
                rows[at, :],
                held[i],
                (((1,), (1 if decoder else 0,)), ((), ())),
                preferred_element_type=f32,
            ).astype(out.dtype)

        @pl.when(jnp.logical_not(live))
        def _():
            out[to, :] = jnp.zeros((TB, FB), out.dtype)

        return carry

    def start_all():
        lax.fori_loop(0, plan.half, start, 0)

    def multiply_all():
        size = plan.half // len(outs)
        for piece, out in enumerate(outs):
            step = functools.partial(multiply, out, piece * size)
            lax.fori_loop(piece * size, (piece + 1) * size, step, 0)

    return start_all, multiply_all


def hbm():
    return pl.BlockSpec(memory_space=pltpu.HBM)


def half_scratch(plan, decoder):
    shape = (FB, plan.columns) if decoder else (plan.columns, FB)
    return [pltpu.VMEM((plan.half, *shape), bf16), pltpu.SemaphoreType.DMA((plan.half,))]


def preact_kernel(plan, own, tab, near, far, weight, *refs):
    outs, (rows, held, row_sem, sems) = refs[:-4], refs[-4:]
    home = tab[plan.pair] if own else 1 - tab[plan.pair]
    moves = [pltpu.make_async_copy(ref, rows, row_sem) for ref in (near, far)]
    for core, move in enumerate(moves):
        pl.when(home == core)(move.start)
    base_row = home * plan.blocks
    start, multiply = half_loop(plan, own, False, tab, rows, base_row, weight, outs, held, sems)
    start()
    moves[0].wait()
    multiply()


def fetch_kernel(plan, tab, weight, held, mark, sems):
    def each(act):
        def one(i, carry):
            @pl.when(tab[plan.live + i] > 0)
            def _():
                act(block_copy(tab, plan.block + i, weight, True, held, sems, i))

            return carry

        lax.fori_loop(0, plan.slots, one, 0)

    each(lambda copy: copy.start())
    each(lambda copy: copy.wait())
    mark[...] = jnp.zeros_like(mark)


def whole():
    return pl.BlockSpec(memory_space=pltpu.VMEM)


def fetch_blocks(plan, tab, weight):
    shape = (plan.slots, FB, plan.columns)
    return plan.launch(
        functools.partial(fetch_kernel, plan),
        "fetch_blocks",
        (1,),
        tab,
        [(weight, hbm())],
        [(pltpu.VMEM(shape, bf16), whole()), (like((8, TB), f32), None)],
        [pltpu.SemaphoreType.DMA((plan.slots,))],
    )[0]


def halves(plan, dtype, count):
    return [(like((plan.half * TB // count, FB), dtype), None)] * count


def preact_half(plan, own, tab, near, far, weight, count):
    held, sems = half_scratch(plan, False)
    return plan.launch(
        functools.partial(preact_kernel, plan, own),
        "preact_half",
        (1,),
        tab,
        [(near, hbm()), (far, hbm()), (weight, hbm())],
        halves(plan, f32 if own else bf16, count),
        [
            pltpu.VMEM((plan.rows, plan.columns), bf16),
            held,
            pltpu.SemaphoreType.DMA,
            sems,
        ],
    )


def act_send_kernel(plan, tab, weight, near, *refs):
    base_row = (1 - tab[plan.pair]) * plan.blocks
    outs, (held, sems) = refs[:-2], refs[-2:]
    start, multiply = half_loop(plan, False, True, tab, near, base_row, weight, outs, held, sems)
    start()
    multiply()


def chunk_rows(plan, chunk):
    return pl.BlockSpec(
        (2 * plan.rows, plan.columns), lambda *_: (chunk, 0), pipeline_mode=pl.Buffered(1)
    )


def act_send(plan, tab, near, weight, after):
    return plan.launch(
        functools.partial(act_send_kernel, plan),
        "act_grad_send",
        (1,),
        tab,
        [(weight, hbm()), (near, None)],
        halves(plan, bf16, 1),
        half_scratch(plan, True),
        after=after,
    )[0]


def act_keep_kernel(plan, count, tab, weight, near, *refs):
    parts, errs, outs = refs[:count], refs[count], refs[count + 1 : -2]
    start, multiply = half_loop(plan, True, True, tab, errs, 0, weight, outs, *refs[-2:])
    start()
    here = pl.multiple_of((1 - tab[plan.pair]) * plan.rows, TB)
    errs[pl.ds(here, plan.rows), :] = near[...]
    size = plan.rows // count
    for i, part in enumerate(parts):
        there = pl.multiple_of(tab[plan.pair] * plan.rows + i * size, GRAIN)
        errs[pl.ds(there, size), :] = part[...]
    multiply()


def act_keep(plan, chunk, tab, near, parts, weight, errs):
    return plan.launch(
        functools.partial(act_keep_kernel, plan, len(parts)),
        "act_grad_keep",
        (1,),
        tab,
        [(weight, hbm()), (near, None)] + [(part, None) for part in parts],
        [
            (like((plan.chips * 2 * plan.rows, plan.columns)), chunk_rows(plan, chunk)),
            *halves(plan, f32, 1),
        ],
        half_scratch(plan, True),
        into=errs,
    )


def pair_sum_kernel(plan, count, tab, keep, *refs):
    recvs, outs = refs[:count], refs[count:]
    size = plan.line // count
    for i, out in enumerate(outs):
        place = tab[plan.place] ^ i
        rows = pl.ds(pl.multiple_of(place * plan.shard, GRAIN), plan.shard)
        for piece, recv in enumerate(recvs):

            @pl.when(place // size == piece)
            def _():
                at = pl.multiple_of((place % size) * plan.shard, GRAIN)
                there = recv[pl.ds(at, plan.shard), :].astype(f32)
                out[...] = (keep[rows, :] + there).astype(out.dtype)


def pair_sum(plan, tab, keep, recvs):
    shape = (plan.shard, FB)
    return plan.launch(
        functools.partial(pair_sum_kernel, plan, len(recvs)),
        "pair_sum",
        (1,),
        tab,
        [(keep, None)] + [(recv, None) for recv in recvs],
        [(like(shape, bf16 if i else f32), None) for i in range(plan.line)],
    )


def grain_slot(plan, tab, grain):
    shard = tab[plan.pair] * plan.line + tab[plan.place]
    slot = (shard * plan.shard + grain * GRAIN) // TB
    return tab[plan.block + slot], tab[plan.live + slot] > 0


def act_kernel(plan, tab, bias, *refs):
    parts, (acts, positives) = refs[:-2], refs[-2:]
    for grain in range(plan.shard // GRAIN):
        block, live = grain_slot(plan, tab, grain)
        rows = slice(grain * GRAIN, (grain + 1) * GRAIN)
        total = bias[pl.ds(block, 1), :]
        for part in parts:
            total = total + part[rows, :].astype(f32)
        positive = jnp.where(live, jnp.maximum(total, 0.0), 0.0)
        positives[rows, :] = positive
        acts[rows, :] = (positive * positive).astype(bf16)


def shard_acts(plan, tab, bias, parts):
    shape = (plan.shard, FB)
    return plan.launch(
        functools.partial(act_kernel, plan),
        "shard_acts",
        (1,),
        tab,
        [(bias, None)] + [(part, None) for part in parts],
        [(like(shape), None), (pltpu.VMEM(shape, f32), None)],
    )


def grad_kernel(plan, tab, norms, positives, *refs):
    parts, out = refs[:-1], refs[-1]
    for grain in range(plan.shard // GRAIN):
        block, live = grain_slot(plan, tab, grain)
        rows = slice(grain * GRAIN, (grain + 1) * GRAIN)
        total = sparsity_weight * norms[pl.ds(block, 1), :]
        for part in parts:
            total = total + part[rows, :].astype(f32)
        out[rows, :] = jnp.where(live, total * 2.0 * positives[rows, :], 0.0).astype(bf16)


def shard_grads(plan, tab, norms, positives, parts):
    return plan.launch(
        functools.partial(grad_kernel, plan),
        "shard_grads",
        (1,),
        tab,
        [(norms, None), (near_memory(positives), None)] + [(part, None) for part in parts],
        [(like((plan.shard, FB)), None)],
    )[0]


def assemble(plan, pair, place, near, far, out, base):
    for side, refs in enumerate((near, far)):
        size = plan.line // len(refs)
        for i in range(plan.line):
            shard = (pair ^ side) * plan.line + (place ^ i)
            at = pl.multiple_of(base + shard * plan.shard, GRAIN)
            part = slice(i % size * plan.shard, (i % size + 1) * plan.shard)
            out[pl.ds(at, plan.shard), :] = refs[i // size][part, :]


def recon_kernel(plan, count, fetched, tab, *refs):
    near, far = refs[:count], refs[count : 2 * count]
    weight, acts, total, *refs = refs[2 * count :]
    others = refs if fetched else refs[:-2]
    held, sems = (weight, None) if fetched else refs[-2:]
    depth = held.shape[0]

    def copy(i):
        return block_copy(tab, plan.block + i, weight, True, held, sems, i % depth)

    def start(i, carry):
        @pl.when(tab[plan.live + i] > 0)
        def _():
            copy(i).start()

        return carry

    def multiply(i, carry):
        @pl.when(tab[plan.live + i] > 0)
        def _():
            at = pl.ds(pl.multiple_of(tab[i] * TB, TB), TB)
            rows = pl.ds(pl.multiple_of(i * TB, TB), TB)
            if not fetched:
                copy(i).wait()
            total[at, :] += jnp.dot(acts[rows, :], held[i % depth], preferred_element_type=f32)

        if not fetched:

            @pl.when(i + depth < plan.slots)
            def _():
                start(i + depth, 0)

        return carry

    if not fetched:
        lax.fori_loop(0, depth, start, 0)
    assemble(plan, tab[plan.pair], tab[plan.place], near, far, acts, 0)
    total[...] = jnp.zeros_like(total)
    lax.fori_loop(0, plan.slots, multiply, 0)
    size = plan.rows // len(others)
    for i, other in enumerate(others):
        at = pl.multiple_of(tab[plan.pair] * plan.rows + i * size, GRAIN)
        other[...] = total[pl.ds(at, size), :].astype(bf16)


def recon(plan, chunk, tab, near, far, weight, acts, pieces, fetched):
    depth = min(DEPTH, plan.slots)
    acts_shape = (plan.slots * TB, FB)
    piece = like((plan.rows // pieces, plan.columns))
    scratch = [pltpu.VMEM((depth, FB, plan.columns), bf16), pltpu.SemaphoreType.DMA((depth,))]
    source = (near_memory(weight), whole()) if fetched else (weight, hbm())
    return plan.launch(
        functools.partial(recon_kernel, plan, len(near), fetched),
        "recon",
        (1,),
        tab,
        [(value, None) for value in (*near, *far)] + [source],
        [
            (
                like((plan.every * TB, FB)),
                pl.BlockSpec(acts_shape, lambda *_: (chunk, 0), pipeline_mode=pl.Buffered(1)),
            ),
            (like((2 * plan.rows, plan.columns), f32), None),
        ]
        + [(piece, None)] * pieces,
        [] if fetched else scratch,
        into=acts,
    )


def column(row):
    return jnp.broadcast_to(row, (TB, row.shape[1])).T[:, :1]


def square_kernel(tab, weight, out, held, sems):
    depth = held.shape[0]

    def copy(i):
        rows = pl.ds(pl.multiple_of(i * FB, FB), FB)
        return pltpu.make_async_copy(weight.at[rows, :], held.at[i % depth], sems.at[i % depth])

    for i in range(depth):
        copy(i).start()

    def add(i, carry):
        copy(i).wait()
        value = held[i % depth].astype(f32)
        total = jnp.sum(value * value, axis=1, keepdims=True)
        out[pl.ds(i, 1), :] = jnp.broadcast_to(total, (FB, TB)).T[:1, :]

        @pl.when(i + depth < LB)
        def _():
            copy(i + depth).start()

        return carry

    lax.fori_loop(0, LB, add, 0)


def square_sums(plan, tab, dec_weight):
    return plan.launch(
        square_kernel,
        "square_sums",
        (1,),
        tab,
        [(dec_weight, hbm())],
        [(like((LB, FB), f32), None)],
        [pltpu.VMEM((DEPTH, FB, plan.columns), bf16), pltpu.SemaphoreType.DMA((DEPTH,))],
    )[0]


def turn_kernel(tab, near, far, out, mark):
    mark[...] = jnp.zeros_like(mark)
    rows = near.shape[0]
    out[:, :rows] = near[...].T
    out[:, rows:] = far[...].T


def turned(plan, chunk, tab, near, far, into):
    width = min(1024, plan.columns)
    block = pl.BlockSpec((plan.rows, width), lambda i, tab: (0, i))
    return plan.launch(
        turn_kernel,
        "turn_rows",
        (plan.columns // width,),
        tab,
        [(near, block), (far, block)],
        [
            (
                pltpu.HBM((plan.columns, plan.chips * 2 * plan.rows), bf16),
                pl.BlockSpec((width, 2 * plan.rows), lambda i, tab: (i, chunk)),
            ),
            (like((8, TB), f32), None),
        ],
        into=into,
    )[0]


def norm_add_kernel(tab, here, there, out):
    out[...] = here[...] + there[...]


def norm_add(plan, tab, here, there):
    return plan.launch(
        norm_add_kernel,
        "norm_add",
        (1,),
        tab,
        [(here, None), (there, None)],
        [(like(here.shape, f32), None)],
    )[0]


def norm_kernel(tab, here, there, total, inverse):
    norm = jnp.sqrt(here[...] + norm_eps)
    total[...] = norm + jnp.sqrt(there[...] + norm_eps)
    inverse[...] = 1.0 / norm


def norms(plan, tab, here, there):
    return plan.launch(
        norm_kernel,
        "norms",
        (1,),
        tab,
        [(here, None), (there, None)],
        [(like(here.shape, f32), None)] * 2,
    )


def two_slots(tab, plan, i, last):
    more = i + 1 < last
    j = jnp.where(more, i + 1, i)

    def at(value):
        return pl.ds(pl.multiple_of(value * TB, TB), TB)

    return more, at(tab[i]), at(tab[j]), at(tab[plan.every + i]), at(tab[plan.every + j])


def grad_dec_kernel(plan, base, tab, inverse, weight, acts, errs, out, mark, total, sums):
    mark[...] = jnp.zeros_like(mark)
    block = base + pl.program_id(0)
    first, last = tab[plan.start + block], tab[plan.start + block + 1]

    def load(i):
        more, here, there, token, other = two_slots(tab, plan, i, last)
        second = jnp.where(more, acts[there, :], jnp.zeros((TB, FB), bf16))
        these = jnp.concatenate([acts[here, :], second], axis=0).T
        rows = jnp.concatenate([errs[token, :], errs[other, :]], axis=0)
        count = jnp.dot(these, jnp.ones((2 * TB, TB), bf16), preferred_element_type=f32)
        return count, jnp.dot(these, rows, preferred_element_type=f32)

    def finish(count, value):
        scale = sparsity_weight * count[:, :1] * column(inverse[pl.ds(block, 1), :])
        out[...] = (value + scale * weight[...].astype(f32)).astype(bf16)

    @pl.when((last > first) & (last - first <= 2))
    def _():
        finish(*load(first))

    @pl.when((last - first > 2) & (last - first <= 4))
    def _():
        count, value = load(first)
        more, rest = load(first + 2)
        finish(count + more, value + rest)

    @pl.when(last - first > 4)
    def _():
        count, value = load(first)
        sums[...] = count
        total[...] = value

        def add(i, carry):
            count, value = load(first + 2 * i)
            sums[...] += count
            total[...] += value
            return carry

        lax.fori_loop(1, (last - first + 1) // 2, add, 0)
        finish(sums[...], total[...])

    @pl.when(first >= last)
    def _():
        out[...] = jnp.zeros(out.shape, bf16)


def grad_dec(plan, base, count, tab, inverse, dec_weight, acts, errs, into=None):
    shape = (FB, plan.columns)
    spec = pl.BlockSpec(shape, lambda i, tab: (base + i, 0))
    return plan.launch(
        functools.partial(grad_dec_kernel, plan, base),
        "grad_dec",
        (count,),
        tab,
        [(inverse, None), (dec_weight, spec), (acts, None), (errs, None)],
        [(like((LB * FB, plan.columns)), spec), (like((8, TB), f32), None)],
        [pltpu.VMEM(shape, f32), pltpu.VMEM((FB, TB), f32)],
        into=into,
    )[0]


def grad_enc_kernel(plan, tab, rows, *refs):
    grads, (out, total, every) = refs[: 2 * plan.chips], refs[2 * plan.chips :]
    block = pl.program_id(0)

    @pl.when(block == 0)
    def _():
        for chunk in range(plan.chips):
            near, far = grads[2 * chunk], grads[2 * chunk + 1]
            base = chunk * plan.slots * TB
            assemble(plan, tab[plan.pair_all], tab[plan.place_all], [near], [far], every, base)

    first, last = tab[plan.start + block], tab[plan.start + block + 1]

    def load(i):
        more, here, there, token, other = two_slots(tab, plan, i, last)
        second = jnp.where(more, every[there, :], jnp.zeros((TB, FB), bf16))
        right = jnp.concatenate([every[here, :], second], axis=0)
        left = jnp.concatenate([rows[:, token], rows[:, other]], axis=1)
        return jnp.dot(left, right, preferred_element_type=f32)

    @pl.when(last - first > 4)
    def _():
        total[...] = load(first)

        def add(i, carry):
            total[...] += load(first + 2 * i)
            return carry

        lax.fori_loop(1, (last - first + 1) // 2, add, 0)
        out[...] = total[...].astype(bf16)

    @pl.when((last > first) & (last - first <= 2))
    def _():
        out[...] = load(first).astype(bf16)

    @pl.when((last - first > 2) & (last - first <= 4))
    def _():
        out[...] = (load(first) + load(first + 2)).astype(bf16)

    @pl.when(last == first)
    def _():
        out[...] = jnp.zeros(out.shape, bf16)


def grad_enc(plan, tab, grads, rows):
    shape = (plan.columns, FB)
    return plan.launch(
        functools.partial(grad_enc_kernel, plan),
        "grad_enc",
        (LB,),
        tab,
        [(value, None) for value in (rows, *grads)],
        [(like((plan.columns, LB * FB)), pl.BlockSpec(shape, lambda i, tab: (0, i)))],
        [pltpu.VMEM(shape, f32), pltpu.VMEM((plan.every * TB, FB), bf16)],
    )[0]


def join_kernel(plan, tab, *refs):
    parts, outs = refs[: plan.line], refs[plan.line :]
    size = plan.line // len(outs)
    for i, part in enumerate(parts):
        rows = slice(i % size * plan.shard, (i % size + 1) * plan.shard)
        outs[i // size][rows, :] = part[...]


def join(plan, tab, parts, count):
    return plan.launch(
        functools.partial(join_kernel, plan),
        "join_shards",
        (1,),
        tab,
        [(part, None) for part in parts],
        halves(plan, bf16, count),
    )


def chip_sum_kernel(plan, tab, both, *refs):
    others, total = refs[:-1], refs[-1]
    size = plan.rows // len(others)
    for i, other in enumerate(others):
        at = pl.multiple_of((1 - tab[plan.pair]) * plan.rows + i * size, GRAIN)
        value = both[pl.ds(at, size), :] + other[...].astype(f32)
        total[i * size : (i + 1) * size, :] = value.astype(bf16)


def chip_sum(plan, tab, both, others):
    return plan.launch(
        functools.partial(chip_sum_kernel, plan),
        "chip_sum",
        (1,),
        tab,
        [(both, None)] + [(other, None) for other in others],
        [(like((plan.rows, plan.columns)), None)],
    )[0]


def error_kernel(plan, pieces, tab, total, bias, near_rows, far_rows, *refs):
    others, near, parts = refs[: -1 - pieces], refs[-1 - pieces], refs[-pieces:]
    size = plan.rows // pieces
    for core, rows in enumerate((near_rows, far_rows)):

        @pl.when(1 - tab[plan.pair] == core)
        def _():
            for i, part in enumerate(parts):
                at = slice(i * size, (i + 1) * size)
                value = total[at, :].astype(f32)
                for other in others:
                    value = value + other[at, :].astype(f32)
                error = value + bias[...] - rows[at, :].astype(f32)
                error = (error * TB ** (-0.5)).astype(bf16)
                near[at, :] = error
                part[...] = error


def errors(plan, tab, total, bias, rows, received, pieces):
    piece = like((plan.rows // pieces, plan.columns))
    return plan.launch(
        functools.partial(error_kernel, plan, pieces),
        "errors",
        (1,),
        tab,
        [(value, None) for value in (total, bias, *rows, *received)],
        [(like(total.shape), None)] + [(piece, None)] * pieces,
    )


def spread_parts(plan, parts):
    return [parts[0]] + [swap(parts[i], "tok", 2 * i) for i in range(1, plan.line)]


def spread_shard(plan, shard):
    return [shard] + [swap(shard, "tok", 2 * i) for i in range(1, plan.line)]


def on_device(resid, enc_weight, enc_bias, dec_weight, dec_bias, active_ids, active_count):
    plan = Plan(lax.axis_size("feat"), lax.axis_size("tok"), *resid.shape)
    chips = range(plan.chips)
    rest = list(chips[1:])
    enc_weight, dec_weight = far_memory(enc_weight), far_memory(dec_weight)
    bias = enc_bias.reshape(LB, FB)
    back = dec_bias[None, :]

    def from_chip(value, chunk):
        return swap(value, "feat", 2 * chunk)

    def both(value):
        return value, swap(value, "feat", 1)

    entries = jnp.where(jnp.arange(K)[None, :] < active_count[:, None], active_ids, -1)
    entries, moving = lax.optimization_barrier((entries, resid))
    lists = {chunk: from_chip(entries, chunk) for chunk in rest}
    tabs = {0: slot_table(plan, both(entries))}
    rows = {0: [far_memory(resid), near_memory(swap(resid, "feat", 1))]}
    arriving = {chunk: from_chip(moving, chunk) for chunk in rest}
    sends, keeps, parts, shards, positives, sums, received, fresh = ({} for _ in range(8))
    turns = acts = errs = None

    def send_products(chunk):
        pieces = preact_half(plan, False, tabs[chunk], *rows[chunk], enc_weight, 1)
        sends[chunk] = [swap(piece, "tok", 1) for piece in pieces]

    def keep_products(chunk):
        keeps[chunk] = preact_half(plan, True, tabs[chunk], *rows[chunk], enc_weight, 1)[0]

    def add_norms(squares, bits):
        for bit in bits:
            squares = norm_add(plan, tabs[0], squares, swap(squares, "tok", bit))
        return squares

    def reduce_pairs(chunk):
        parts[chunk] = spread_parts(plan, pair_sum(plan, tabs[chunk], keeps[chunk], sends[chunk]))

    def activate(chunk):
        shard, positives[chunk] = shard_acts(plan, tabs[chunk], bias, parts[chunk])
        shards[chunk] = spread_shard(plan, shard)

    def gather(chunk, count=1):
        near = join(plan, tabs[chunk], shards[chunk], count)
        shards[chunk] = (near, [swap(piece, "tok", 1) for piece in near])

    def rebuild(chunk, acts):
        count, weight = (4 if chunk else 1), dec_weight
        if chunk:
            weight = fetch_blocks(plan, tabs[chunk], dec_weight)
        acts, both, *others = recon(
            plan, chunk, tabs[chunk], *shards[chunk], weight, acts, count, chunk > 0
        )
        sums[chunk] = (both, others)
        return acts

    def total(chunk):
        own, others = sums[chunk]
        others = [swap(plan.pin(other), "feat", 1) for other in others]
        sums[chunk] = chip_sum(plan, tabs[chunk], own, others)
        for step in rest:
            received[chunk ^ step, step] = from_chip(sums[chunk], step)

    def compare(chunk):
        others = [received[chunk, step] for step in rest]
        near, *pieces = errors(plan, tabs[chunk], sums[chunk], back, rows[chunk], others, 4 if chunk else 1)
        fresh[chunk] = (near, pieces)

    def back_send(chunk):
        near, parts = fresh[chunk]
        fresh[chunk] = (near, [swap(plan.pin(part), "feat", 1) for part in parts])
        after = fresh[chunk][1] if chunk else ()
        sends[chunk] = [swap(act_send(plan, tabs[chunk], near, dec_weight, after), "tok", 1)]

    def back_keep(chunk, errs):
        errs, keeps[chunk] = act_keep(plan, chunk, tabs[chunk], *fresh[chunk], dec_weight, errs)
        return errs

    def differentiate(chunk):
        shard = shard_grads(plan, tabs[chunk], norm_sum, positives[chunk], parts[chunk])
        shards[chunk] = spread_shard(plan, shard)

    bits = [1 << i for i in range((plan.toks - 1).bit_length())]
    send_products(0)
    keep_products(0)
    squares = square_sums(plan, tabs[0], dec_weight)
    reduce_pairs(0)
    for chunk in rest:
        tabs[chunk] = slot_table(plan, both(plan.pin(lists[chunk])))
    activate(0)
    for chunk in rest:
        rows[chunk] = [near_memory(value) for value in both(plan.pin(arriving[chunk]))]
        send_products(chunk)
        keep_products(chunk)
    gather(0)
    for chunk in chips:
        turns = turned(plan, chunk, tabs[chunk], *rows[chunk], turns)
    for chunk in rest:
        reduce_pairs(chunk)
    acts = rebuild(0, acts)
    for chunk in rest:
        activate(chunk)
    total(0)
    for chunk in rest:
        gather(chunk)
    squares = add_norms(squares, bits[1:-1])
    order = order_table(plan, [tabs[chunk] for chunk in chips])
    for chunk in rest:
        acts = rebuild(chunk, acts)
    squares = add_norms(squares, bits[:1])
    for chunk in rest:
        total(chunk)

    for chunk in rest:
        compare(chunk)
        back_send(chunk)
        errs = back_keep(chunk, errs)
    norm_sum, inverse = norms(plan, tabs[0], squares, swap(squares, "tok", bits[-1]))
    for chunk in rest:
        reduce_pairs(chunk)
    compare(0)
    for chunk in rest:
        differentiate(chunk)
    back_send(0)
    errs = back_keep(0, errs)
    reduce_pairs(0)
    values = (order, inverse, dec_weight, acts, errs)
    out_dec = grad_dec(plan, 0, 4, *values)
    for chunk in rest:
        gather(chunk)
    differentiate(0)
    out_dec = grad_dec(plan, 4, 4, *values, into=out_dec)
    gather(0)
    out_dec = grad_dec(plan, 8, LB - 8, *values, into=out_dec)
    out_enc = grad_enc(plan, order, [side[0] for chunk in chips for side in shards[chunk]], near_memory(turns))
    return (out_enc, out_dec)


def solution(mesh):
    return jax.shard_map(
        on_device,
        mesh=mesh,
        in_specs=(
            P("feat", "tok"),
            P("tok", "feat"),
            P("feat"),
            P("feat", "tok"),
            P("tok"),
            P("feat", None),
            P("feat"),
        ),
        out_specs=(P("tok", "feat"), P("feat", "tok")),
        check_vma=False,
    )
```
